768 devices in a mesh: ctx: 16 (over z_hi, x), chan: 48 (over z_lo, y, core).
Axes of the slice: x: 4, y: 8, z: 12 (z_hi: 4, z_lo: 3; z = z_hi * 3 + z_lo), core: 2. Of those that a mesh axis runs over, the one named last changes fastest.
Arguments:
- query_gate: float32 [768, 131072], P('chan', 'ctx'), parts along dimension 0, may hold values from -6 to 6
- key_gate: float32 [768, 131072], P('chan', 'ctx'), parts along dimension 0, may hold values from -6 to 6
- value_rows: float32 [768, 131072], P('chan', 'ctx'), parts along dimension 0, may hold values from -6 to 6
- filter_index: int32 [768], P('chan'), parts along dimension 0, may hold values from 0 to 47
- residues: float32 [48, 16], replicated, may hold values from -1.5 to 1.5
- decay_rates: float32 [48, 16], replicated, may hold values from 7.6293945e-06 to 0.1
- skip_gain: float32 [768], P('chan'), parts along dimension 0, may hold values from 0.5 to 1.5
Outputs:
- mixed_out: float32 [768, 131072], P('chan', 'ctx'), parts along dimension 0
The draws below stay inside these ranges and needn't reach their ends.
There are 48 independent parts, one for each index of `chan`. The reference program is written for one: setup_inputs(seed, part) draws one part's arguments, and reference() takes and returns one part's arrays. A program takes and returns all parts, laid end to end along the dimension named above; an argument that names none is the same for every part. Nothing has to cross between parts.
Inputs may be any that keep to these rules, and one draw needn't show every extreme that they name: `filter_index`: each channel names one of the 48 filters.
All inputs are finite; a program needn't handle non-finite values.
Results may differ from the reference program's by a relative error of at most 0.000071.
Values sent between devices are 32-bit elements; how exact they have to be, the bound alone decides.
No kernel may reach another device: no remote copies, remote signals or barrier semaphores. Data moves between devices by JAX's collectives and lax.ppermute only.
A program may use at most 32 MiB of HBM per device.

```python
import math
import jax
import jax.numpy as jnp
from jax import lax

CH = 16
FILTERS = 48
MODES = 16
SEQ = 131072
FFT_LEN = 262144


def set_ends(result, own_key, smallest, top_value):
    shape = result.shape
    place = [jax.random.randint(jax.random.fold_in(own_key, axis), (), 0, shape[axis]) for axis in range(len(shape))]
    result = result.at[tuple(place)].set(smallest)
    longest = shape.index(max(shape))
    place[longest] = (place[longest] + 1) % shape[longest]
    return result.at[tuple(place)].set(top_value)


def block_levels(stream_key, dims, split, least, largest):
    level, own = 1.0, jax.random.fold_in(stream_key, 6)
    for position, parts in split:
        steps = jnp.exp(jax.random.uniform(jax.random.fold_in(own, position), (parts,), jnp.float32, least / len(split), largest / len(split)))
        level = level * jnp.repeat(steps, dims[position] // parts).reshape([-1 if axis == position else 1 for axis in range(len(dims))])
    return level


def gaussian(own_key, shape, deviation, most, cuts=(), kind=jnp.bfloat16):
    entries = deviation * jax.random.normal(own_key, shape, jnp.float32)
    if cuts:
        entries = entries * block_levels(own_key, shape, cuts, -0.22, 0.18)
    return jnp.clip(entries, -most, most).astype(kind)


def setup_inputs(seed: int = 0, part: int = 0) -> dict:
    seeds = jax.random.split(jax.random.key(seed), 8)
    part_keys = jax.random.split(jax.random.fold_in(seeds[7], part), 8)
    return {
        "query_gate": gaussian(part_keys[0], (CH, SEQ), 1.0, 6.0, ((1, 16),), jnp.float32),
        "key_gate": gaussian(part_keys[1], (CH, SEQ), 1.0, 6.0, ((1, 16),), jnp.float32),
        "value_rows": gaussian(part_keys[2], (CH, SEQ), 1.0, 6.0, ((1, 16),), jnp.float32),
        "filter_index": set_ends(jax.random.randint(part_keys[3], (CH,), 0, FILTERS), jax.random.fold_in(part_keys[3], 1), 0, FILTERS - 1).astype(jnp.int32),
        "residues": gaussian(seeds[4], (FILTERS, MODES), 0.25, 1.5, (), jnp.float32),
        "decay_rates": jnp.clip(jnp.exp(jax.random.uniform(seeds[5], (FILTERS, MODES), jnp.float32, math.log(7.62939453125e-06), math.log(0.1))), 7.62939453125e-06, 0.1),
        "skip_gain": jnp.clip(1.0 + 0.1 * jax.random.normal(part_keys[6], (CH,), jnp.float32), 0.5, 1.5),
    }


def spectrum(freq_index, rate_modes, weight_modes, seqlen, period):
    signed = jnp.where(2 * freq_index < period, freq_index, freq_index - period)
    theta_tab = signed.astype(jnp.float32) * (2.0 * math.pi / period)
    parity = 1.0 - 2.0 * (freq_index % 2).astype(jnp.float32)
    half_sin = jnp.sin(0.5 * theta_tab)
    sinus = jnp.sin(theta_tab)
    bcast_shape = (rate_modes.shape[0],) + (1,) * freq_index.ndim

    def add_mode(mode_id, sums_now):
        real_sum, imag_sum = sums_now
        decay_now = lax.dynamic_index_in_dim(rate_modes, mode_id, 1, keepdims=False).reshape(bcast_shape)
        weight_now = lax.dynamic_index_in_dim(weight_modes, mode_id, 1, keepdims=False).reshape(bcast_shape)
        fade_now = jnp.exp(-decay_now)
        mode_gain = weight_now * jnp.sqrt(-jnp.expm1(-2.0 * decay_now))
        numerator = mode_gain * (1.0 - jnp.exp(-decay_now * seqlen) * parity)
        den_re = -jnp.expm1(-decay_now) + 2.0 * fade_now * half_sin * half_sin
        den_im = fade_now * sinus
        inverse = numerator / (den_re * den_re + den_im * den_im)
        return (real_sum + inverse * den_re, imag_sum - inverse * den_im)
    zero_sums = jnp.zeros((rate_modes.shape[0],) + freq_index.shape, jnp.float32)
    return lax.fori_loop(0, rate_modes.shape[1], add_mode, (zero_sums, zero_sums))

def reference(query_gate, key_gate, value_rows, filter_index, residues, decay_rates, skip_gain):
    mixed_kv = key_gate.astype(jnp.float32) * value_rows.astype(jnp.float32)
    onehot = (filter_index[:, None] == jnp.arange(FILTERS, dtype=jnp.int32)[None, :]).astype(jnp.float32)
    weights = jnp.dot(onehot, residues, precision=lax.Precision.HIGHEST)
    rate_modes = jnp.dot(onehot, decay_rates, precision=lax.Precision.HIGHEST)
    freq_index = jnp.arange(FFT_LEN, dtype=jnp.int32)
    filt_re, filt_im = spectrum(freq_index, rate_modes, weights, SEQ, FFT_LEN)
    padded = jnp.concatenate([mixed_kv, jnp.zeros_like(mixed_kv)], axis=1)
    signal_freq = jnp.fft.fft(padded, axis=1)
    conv_out = jnp.real(jnp.fft.ifft(signal_freq * (filt_re + 1j * filt_im), axis=1))[:, :SEQ]
    return query_gate.astype(jnp.float32) * (conv_out + skip_gain[:, None] * mixed_kv)
```

```python
import jax
import jax.numpy as jnp
from jax import lax
from jax.experimental import pallas as pl
from jax.experimental.pallas import tpu as pltpu
from jax.sharding import PartitionSpec as P

BLOCK = 128
HALF = 8
F32, BF16 = jnp.float32, jnp.bfloat16
NN = (((1,), (0,)), ((), ()))
NT = (((1,), (1,)), ((), ()))


def split(value):
    high = value.astype(BF16)
    return high, (value - high.astype(F32)).astype(BF16)


def iota(shape, dim):
    return lax.broadcasted_iota(jnp.int32, shape, dim)


def lanes_of(table, modes):
    channels = table.shape[0]
    spread_shape = (modes, channels * modes)
    spread = (iota(spread_shape, 1) % modes == iota(spread_shape, 0)).astype(F32)
    wide = lax.dot_general(table, spread, NN, precision=lax.Precision.HIGHEST, preferred_element_type=F32)
    own = iota(wide.shape, 1) // modes == iota(wide.shape, 0)
    return jnp.sum(jnp.where(own, wide, 0.0), axis=0, keepdims=True)


def one_minus_exp(x):
    series = jnp.full_like(x, 1.0)
    for k in range(9, 1, -1):
        series = 1.0 - x * series * (1.0 / k)
    return jnp.where(x <= 0.25, x * series, 1.0 - jnp.exp(-x))


def state_kernel(index_ref, rates_ref, residues_ref, key_ref, value_ref, end_ref, rate_ref, gain_ref, rate_rows, weight_rows):
    channels, modes = rate_rows.shape
    blocks = key_ref.shape[1] // BLOCK
    for c in range(channels):
        rate_rows[c : c + 1, :] = rates_ref[pl.ds(index_ref[c], 1), :]
        weight_rows[c : c + 1, :] = residues_ref[pl.ds(index_ref[c], 1), :]
    rates = rate_rows[...]
    gains = weight_rows[...] * jnp.sqrt(one_minus_exp(2.0 * rates))
    rate_row = lanes_of(rates, modes)
    gain_row = lanes_of(gains, modes)
    own = iota((HALF, BLOCK), 1) // modes == iota((HALF, BLOCK), 0)
    for g in range(channels // HALF):
        lanes = slice(g * BLOCK, (g + 1) * BLOCK)
        rate = rate_row[:, lanes]
        rate_ref[g : g + 1, :] = rate
        gain_ref[g : g + 1, :] = gain_row[:, lanes]
        to_end = (BLOCK - 1 - iota((BLOCK, BLOCK), 0)).astype(F32)
        fade_high, fade_low = split(jnp.exp(-rate * to_end))
        fades = jnp.concatenate([fade_high, fade_high, fade_low], axis=0)
        later = (BLOCK * (blocks - 1 - iota((blocks, BLOCK), 0))).astype(F32)
        block_fade = jnp.exp(-rate * later)
        rows = slice(g * HALF, (g + 1) * HALF)
        total = jnp.zeros((HALF, BLOCK), F32)
        for start in range(0, blocks, 16):
            mixed = jnp.concatenate(
                [
                    key_ref[rows, b * BLOCK : (b + 1) * BLOCK] * value_ref[rows, b * BLOCK : (b + 1) * BLOCK]
                    for b in range(start, start + 16)
                ],
                axis=0,
            )
            high, low = split(mixed)
            states = lax.dot_general(
                jnp.concatenate([high, low, high], axis=1), fades, NN, preferred_element_type=F32
            )
            for b in range(16):
                total = total + block_fade[start + b : start + b + 1, :] * states[b * HALF : (b + 1) * HALF, :]
        end_ref[g : g + 1, :] = jnp.sum(jnp.where(own, total, 0.0), axis=0, keepdims=True)


def output_kernel(modes, query_ref, key_ref, value_ref, skip_ref, rate_ref, gain_ref, carried_ref, out_ref, mixed_rows, conv_rows, carry_rows):
    channels = query_ref.shape[0]
    blocks = key_ref.shape[1] // BLOCK
    own = iota((HALF, BLOCK), 1) // modes == iota((HALF, BLOCK), 0)
    own_gain = iota((channels, BLOCK), 1) // modes
    square = (BLOCK, BLOCK)
    causal = iota(square, 1) >= iota(square, 0)
    for g in range(channels // HALF):
        rows = slice(g * HALF, (g + 1) * HALF)
        rate, gain = rate_ref[g : g + 1, :], gain_ref[g : g + 1, :]
        place = iota(square, 0).astype(F32)
        tail = gain * jnp.exp(-rate * place)
        sums = (iota((HALF, BLOCK), 1) // modes == iota((HALF, BLOCK), 0)).astype(F32)
        taps = lax.dot_general(sums, tail, NT, precision=lax.Precision.HIGHEST, preferred_element_type=F32)
        to_end = BLOCK - 1.0 - place
        fade_high, fade_low = split(jnp.exp(-rate * to_end))
        fades = jnp.concatenate([fade_high, fade_high, fade_low], axis=0)
        lead_high, lead_low = split(tail * jnp.exp(-rate))
        leads = jnp.concatenate([lead_high, lead_high, lead_low], axis=1)
        step = jnp.exp(-rate * float(BLOCK))
        state = jnp.broadcast_to(carried_ref[g : g + 1, :], (HALF, BLOCK))
        for start in range(0, blocks, 16):
            mixed = jnp.concatenate(
                [
                    key_ref[rows, b * BLOCK : (b + 1) * BLOCK] * value_ref[rows, b * BLOCK : (b + 1) * BLOCK]
                    for b in range(start, start + 16)
                ],
                axis=0,
            )
            mixed_rows[start * HALF : (start + 16) * HALF, :] = mixed
            high, low = split(mixed)
            states = lax.dot_general(
                jnp.concatenate([high, low, high], axis=1), fades, NN, preferred_element_type=F32
            )
            entering = []
            for b in range(16):
                entering.append(jnp.where(own, state, 0.0))
                state = state * step + states[b * HALF : (b + 1) * HALF, :]
            high, low = split(jnp.concatenate(entering, axis=0))
            carry_rows[start * HALF : (start + 16) * HALF, :] = lax.dot_general(
                jnp.concatenate([high, low, high], axis=1), leads, NT, preferred_element_type=F32
            )
        for c in range(HALF):
            shifted = pltpu.roll(jnp.broadcast_to(taps[c : c + 1, :], square), 0, 1, stride=1, stride_axis=0)
            tap_high, tap_low = split(jnp.where(causal, shifted, 0.0))
            weights = jnp.concatenate([tap_high, tap_high, tap_low], axis=0)
            high, low = split(mixed_rows[pl.ds(c, blocks, stride=HALF), :])
            conv_rows[pl.ds(c, blocks, stride=HALF), :] = lax.dot_general(
                jnp.concatenate([high, low, high], axis=1), weights, NN, preferred_element_type=F32
            )
        skip = skip_ref[rows, :]
        for b in range(blocks):
            here = slice(b * HALF, (b + 1) * HALF)
            lanes = slice(b * BLOCK, (b + 1) * BLOCK)
            conv = conv_rows[here, :] + carry_rows[here, :] + skip * mixed_rows[here, :]
            out_ref[rows, lanes] = query_ref[rows, lanes] * conv


VMEM = pl.BlockSpec(memory_space=pltpu.VMEM)


def per_device(query_gate, key_gate, value_rows, filter_index, residues, decay_rates, skip_gain):
    channels, length = key_gate.shape
    modes = residues.shape[1]
    blocks = length // BLOCK
    groups = channels // HALF
    row = jax.ShapeDtypeStruct((groups, BLOCK), F32)
    ends, rate, gain = pl.pallas_call(
        state_kernel,
        out_shape=(row, row, row),
        in_specs=[pl.BlockSpec(memory_space=pltpu.SMEM)] + [VMEM] * 4,
        out_specs=(VMEM, VMEM, VMEM),
        scratch_shapes=[pltpu.VMEM((channels, modes), F32), pltpu.VMEM((channels, modes), F32)],
        compiler_params=pltpu.CompilerParams(vmem_limit_bytes=16 * 2**20),
        cost_estimate=pl.CostEstimate(flops=2 * 3 * 1024 * 128 * 128, bytes_accessed=2**20, transcendentals=2**16),
    )(filter_index, decay_rates, residues, key_gate, value_rows)

    devices = lax.axis_size("ctx")
    here = lax.axis_index("ctx")
    copies = jnp.broadcast_to(ends.reshape(1, 1, -1), (devices, 1, ends.size))
    every = lax.all_to_all(copies, "ctx", split_axis=0, concat_axis=0, tiled=True).reshape(devices, groups, BLOCK)
    distance = (here - 1 - jnp.arange(devices, dtype=jnp.int32)).astype(F32)[:, None, None]
    fade = jnp.where(distance >= 0.0, jnp.exp(-rate[None] * float(length) * jnp.maximum(distance, 0.0)), 0.0)
    carried = jnp.sum(fade * every, axis=0)

    rows = pltpu.VMEM((blocks * HALF, BLOCK), F32)
    return pl.pallas_call(
        lambda *refs: output_kernel(modes, *refs),
        out_shape=jax.ShapeDtypeStruct(query_gate.shape, F32),
        in_specs=[VMEM] * 7,
        out_specs=VMEM,
        scratch_shapes=[rows, rows, rows],
        compiler_params=pltpu.CompilerParams(vmem_limit_bytes=24 * 2**20),
        cost_estimate=pl.CostEstimate(flops=2 * 9 * 1024 * 128 * 128, bytes_accessed=2**21, transcendentals=2**16),
    )(query_gate, key_gate, value_rows, skip_gain[:, None], rate, gain, carried)


def solution(mesh):
    placed = (P("chan", "ctx"), P("chan", "ctx"), P("chan", "ctx"), P("chan"), P(), P(), P("chan"))
    return jax.shard_map(
        per_device, mesh=mesh, in_specs=placed, out_specs=P("chan", "ctx"), check_vma=False
    )
```

```python
import jax
import jax.numpy as jnp
from jax import lax
from jax.experimental import pallas as pl
from jax.experimental.pallas import tpu as pltpu
from jax.sharding import PartitionSpec as P

BLOCK = 128
HALF = 8
F32, BF16 = jnp.float32, jnp.bfloat16
NN = (((1,), (0,)), ((), ()))
NT = (((1,), (1,)), ((), ()))


def split(value):
    high = value.astype(BF16)
    return high, (value - high.astype(F32)).astype(BF16)


def iota(shape, dim):
    return lax.broadcasted_iota(jnp.int32, shape, dim)


def one_minus_exp(x):
    series = jnp.full_like(x, 1.0)
    for k in range(9, 1, -1):
        series = 1.0 - x * series * (1.0 / k)
    return jnp.where(x <= 0.25, x * series, 1.0 - jnp.exp(-x))


def state_kernel(
    side, index_hbm, rates_hbm, residues_hbm, skip_hbm, key_hbm, value_hbm, query_hbm,
    end_ref, rate_ref, gain_ref, far_ref, row_ref, before_ref, skip_ref, mixed_ref, query_ref,
    index_ref, rates_ref, residues_ref, skip_row, key_ref, value_ref, sems,
):
    channels, length = key_ref.shape
    modes, filters = rates_ref.shape
    blocks = length // BLOCK
    groups = channels // HALF
    small = [
        pltpu.make_async_copy(source, target, sems.at[2 * groups + 1 + i])
        for i, (source, target) in enumerate(
            ((index_hbm, index_ref), (rates_hbm, rates_ref), (residues_hbm, residues_ref), (skip_hbm, skip_row))
        )
    ]
    for copy in small:
        copy.start()
    loads = []
    for g in range(groups):
        rows = slice(g * HALF, (g + 1) * HALF)
        pair = [
            pltpu.make_async_copy(source.at[rows, :], target.at[rows, :], sems.at[2 * g + i])
            for i, (source, target) in enumerate(((key_hbm, key_ref), (value_hbm, value_ref)))
        ]
        for copy in pair:
            copy.start()
        loads.append(pair)
    query_load = pltpu.make_async_copy(query_hbm, query_ref, sems.at[2 * groups])
    query_load.start()
    for copy in small:
        copy.wait()

    wide = (channels, channels * modes)
    spread = (iota(wide, 1) // modes == iota(wide, 0)).astype(BF16)
    chosen = (iota((filters, channels), 0) == index_ref[...]).astype(BF16)
    chosen = lax.dot_general(chosen, spread, NN, preferred_element_type=F32)
    own_mode = iota((modes, channels * modes), 1) % modes == iota((modes, channels * modes), 0)

    def lanes_of(table):
        spread_table = lax.dot_general(
            table, chosen, NN, precision=lax.Precision.HIGHEST, preferred_element_type=F32
        )
        return jnp.sum(jnp.where(own_mode, spread_table, 0.0), axis=0, keepdims=True)

    rate_row = lanes_of(rates_ref[...])
    gain_row = lanes_of(residues_ref[...]) * jnp.sqrt(one_minus_exp(2.0 * rate_row))
    own = iota((HALF, BLOCK), 1) // modes == iota((HALF, BLOCK), 0)
    place = lax.axis_index("ctx") % side
    same = iota((channels, channels), 0) == iota((channels, channels), 1)
    skip = jnp.sum(jnp.where(same, skip_row[...], 0.0), axis=1, keepdims=True)
    skip_ref[...] = jnp.broadcast_to(skip, skip_ref.shape)
    for g in range(groups):
        lanes = slice(g * BLOCK, (g + 1) * BLOCK)
        rate = rate_row[:, lanes]
        here = slice(g, g + 1)
        rate_ref[here, :] = rate
        gain_ref[here, :] = gain_row[:, lanes]
        passed = -rate * float(length)
        far_ref[0, here, :] = jnp.exp(passed * float(side))
        far_ref[1, here, :] = jnp.exp(passed * place.astype(F32))
        for x in range(side):
            row_ref[x, here, :] = jnp.exp(passed * float(side - 1 - x))
            gap = (place - 1 - x).astype(F32)
            before_ref[x, here, :] = jnp.where(gap >= 0.0, jnp.exp(passed * jnp.maximum(gap, 0.0)), 0.0)
        to_end = (BLOCK - 1 - iota((BLOCK, BLOCK), 0)).astype(F32)
        fade_high, fade_low = split(jnp.exp(-rate * to_end))
        fades = jnp.concatenate([fade_high, fade_high, fade_low], axis=0)
        later = (BLOCK * (blocks - 1 - iota((blocks, BLOCK), 0))).astype(F32)
        block_fade = jnp.exp(-rate * later)
        rows = slice(g * HALF, (g + 1) * HALF)
        total = jnp.zeros((HALF, BLOCK), F32)
        for copy in loads[g]:
            copy.wait()
        for start in range(0, blocks, 16):
            mixed = jnp.concatenate(
                [
                    key_ref[rows, b * BLOCK : (b + 1) * BLOCK] * value_ref[rows, b * BLOCK : (b + 1) * BLOCK]
                    for b in range(start, start + 16)
                ],
                axis=0,
            )
            mixed_ref[g, start * HALF : (start + 16) * HALF, :] = mixed
            high, low = split(mixed)
            states = lax.dot_general(
                jnp.concatenate([high, low, high], axis=1), fades, NN, preferred_element_type=F32
            )
            for b in range(16):
                total = total + block_fade[start + b : start + b + 1, :] * states[b * HALF : (b + 1) * HALF, :]
        end_ref[here, :] = jnp.sum(jnp.where(own, total, 0.0), axis=0, keepdims=True)
    query_load.wait()


def output_kernel(
    modes, query_ref, mixed_ref, skip_ref, rate_ref, gain_ref, far_ref, near_ref, carried_ref, out_ref, conv_rows, carry_rows
):
    channels, length = query_ref.shape
    blocks = length // BLOCK
    own = iota((HALF, BLOCK), 1) // modes == iota((HALF, BLOCK), 0)
    square = (BLOCK, BLOCK)
    causal = iota(square, 1) >= iota(square, 0)
    for g in range(channels // HALF):
        rows = slice(g * HALF, (g + 1) * HALF)
        here = slice(g, g + 1)
        rate, gain = rate_ref[here, :], gain_ref[here, :]
        place = iota(square, 0).astype(F32)
        tail = gain * jnp.exp(-rate * place)
        taps = lax.dot_general(
            own.astype(F32), tail, NT, precision=lax.Precision.HIGHEST, preferred_element_type=F32
        )
        to_end = BLOCK - 1.0 - place
        fade_high, fade_low = split(jnp.exp(-rate * to_end))
        fades = jnp.concatenate([fade_high, fade_high, fade_low], axis=0)
        lead_high, lead_low = split(tail * jnp.exp(-rate))
        leads = jnp.concatenate([lead_high, lead_high, lead_low], axis=1)
        step = jnp.exp(-rate * float(BLOCK))
        entered = near_ref[here, :] + far_ref[1, here, :] * carried_ref[here, :]
        state = jnp.broadcast_to(entered, (HALF, BLOCK))
        for start in range(0, blocks, 16):
            some = slice(start * HALF, (start + 16) * HALF)
            high, low = split(mixed_ref[g, some, :])
            states = lax.dot_general(
                jnp.concatenate([high, low, high], axis=1), fades, NN, preferred_element_type=F32
            )
            entering = []
            for b in range(16):
                entering.append(jnp.where(own, state, 0.0))
                state = state * step + states[b * HALF : (b + 1) * HALF, :]
            high, low = split(jnp.concatenate(entering, axis=0))
            carry_rows[some, :] = lax.dot_general(
                jnp.concatenate([high, low, high], axis=1), leads, NT, preferred_element_type=F32
            )
        for c in range(HALF):
            shifted = pltpu.roll(jnp.broadcast_to(taps[c : c + 1, :], square), 0, 1, stride=1, stride_axis=0)
            tap_high, tap_low = split(jnp.where(causal, shifted, 0.0))
            weights = jnp.concatenate([tap_high, tap_high, tap_low], axis=0)
            high, low = split(mixed_ref[g, pl.ds(c, blocks, stride=HALF), :])
            conv_rows[pl.ds(c, blocks, stride=HALF), :] = lax.dot_general(
                jnp.concatenate([high, low, high], axis=1), weights, NN, preferred_element_type=F32
            )
        skip = skip_ref[rows, :]
        for b in range(blocks):
            some = slice(b * HALF, (b + 1) * HALF)
            lanes = slice(b * BLOCK, (b + 1) * BLOCK)
            conv = conv_rows[some, :] + carry_rows[some, :] + skip * mixed_ref[g, some, :]
            out_ref[rows, lanes] = query_ref[rows, lanes] * conv


VMEM = pl.BlockSpec(memory_space=pltpu.VMEM)
HBM = pl.BlockSpec(memory_space=pltpu.HBM)
SIDE = 4


def shape(*dims):
    return jax.ShapeDtypeStruct(dims, F32)


def per_device(query_gate, key_gate, value_rows, filter_index, residues, decay_rates, skip_gain):
    channels, length = key_gate.shape
    modes = residues.shape[1]
    blocks = length // BLOCK
    groups = channels // HALF
    line = (groups, BLOCK)
    ends, rate, gain, far, in_row, before, skip, mixed, query = pl.pallas_call(
        lambda *refs: state_kernel(SIDE, *refs),
        out_shape=(
            shape(*line), shape(*line), shape(*line), shape(2, *line), shape(SIDE, *line), shape(SIDE, *line),
            shape(channels, BLOCK), shape(groups, blocks * HALF, BLOCK), shape(channels, length),
        ),
        in_specs=[HBM] * 7,
        out_specs=(VMEM,) * 9,
        scratch_shapes=[
            pltpu.VMEM((1, channels), jnp.int32),
            pltpu.VMEM((modes, residues.shape[0]), F32),
            pltpu.VMEM((modes, residues.shape[0]), F32),
            pltpu.VMEM((1, channels), F32),
            pltpu.VMEM((channels, length), F32),
            pltpu.VMEM((channels, length), F32),
            pltpu.SemaphoreType.DMA((2 * groups + 5,)),
        ],
        compiler_params=pltpu.CompilerParams(vmem_limit_bytes=16 * 2**20),
        cost_estimate=pl.CostEstimate(flops=2 * 3 * 1024 * 128 * 128, bytes_accessed=2**20, transcendentals=2**16),
    )(
        *(
            pltpu.with_memory_space_constraint(array, pltpu.HBM)
            for array in (
                filter_index.reshape(1, channels), decay_rates.T, residues.T, skip_gain.reshape(1, channels),
                key_gate, value_rows, query_gate,
            )
        )
    )

    rows = lax.axis_size("ctx") // SIDE
    every = lax.all_gather(ends, "ctx", axis_index_groups=[[r * SIDE + x for x in range(SIDE)] for r in range(rows)])
    total = jnp.sum(in_row * every, axis=0)
    near = jnp.sum(before * every, axis=0)
    carried = jnp.zeros(line, F32)
    for r in range(rows - 1):
        sent = total + far[0] * carried if r else total
        pairs = [(r * SIDE + x, (r + 1) * SIDE + x) for x in range(SIDE)]
        carried = carried + lax.ppermute(sent, "ctx", pairs)

    stripe = pltpu.VMEM((blocks * HALF, BLOCK), F32)
    return pl.pallas_call(
        lambda *refs: output_kernel(modes, *refs),
        out_shape=shape(channels, length),
        in_specs=[VMEM] * 8,
        out_specs=VMEM,
        scratch_shapes=[stripe, stripe],
        compiler_params=pltpu.CompilerParams(vmem_limit_bytes=24 * 2**20),
        cost_estimate=pl.CostEstimate(flops=2 * 9 * 1024 * 128 * 128, bytes_accessed=2**21, transcendentals=2**16),
    )(query, mixed, skip, rate, gain, far, near, carried)


def solution(mesh):
    placed = (P("chan", "ctx"), P("chan", "ctx"), P("chan", "ctx"), P("chan"), P(), P(), P("chan"))
    return jax.shard_map(
        per_device, mesh=mesh, in_specs=placed, out_specs=P("chan", "ctx"), check_vma=False
    )
```

```python
import jax
import jax.numpy as jnp
from jax import lax
from jax.experimental import pallas as pl
from jax.experimental.pallas import tpu as pltpu
from jax.sharding import PartitionSpec as P

BLOCK = 128
HALF = 8
F32, BF16 = jnp.float32, jnp.bfloat16
NN = (((1,), (0,)), ((), ()))
NT = (((1,), (1,)), ((), ()))


def split(value):
    high = value.astype(BF16)
    return high, (value - high.astype(F32)).astype(BF16)


def iota(shape, dim):
    return lax.broadcasted_iota(jnp.int32, shape, dim)


def one_minus_exp(x):
    series = jnp.full_like(x, 1.0)
    for k in range(9, 1, -1):
        series = 1.0 - x * series * (1.0 / k)
    return jnp.where(x <= 0.25, x * series, 1.0 - jnp.exp(-x))


def state_kernel(
    side, index_hbm, rates_hbm, residues_hbm, skip_hbm, key_hbm, value_hbm, query_hbm,
    end_ref, rate_ref, gain_ref, far_ref, pair_ref, row_ref, skip_ref, mixed_ref, state_ref, query_ref,
    index_ref, rates_ref, residues_ref, skip_row, key_ref, value_ref, sems,
):
    channels, length = key_ref.shape
    modes, filters = rates_ref.shape
    blocks = length // BLOCK
    groups = channels // HALF
    small = [
        pltpu.make_async_copy(source, target, sems.at[2 * groups + 1 + i])
        for i, (source, target) in enumerate(
            ((index_hbm, index_ref), (rates_hbm, rates_ref), (residues_hbm, residues_ref), (skip_hbm, skip_row))
        )
    ]
    for copy in small:
        copy.start()
    loads = []
    for g in range(groups):
        rows = slice(g * HALF, (g + 1) * HALF)
        pair = [
            pltpu.make_async_copy(source.at[rows, :], target.at[rows, :], sems.at[2 * g + i])
            for i, (source, target) in enumerate(((key_hbm, key_ref), (value_hbm, value_ref)))
        ]
        for copy in pair:
            copy.start()
        loads.append(pair)
    query_load = pltpu.make_async_copy(query_hbm, query_ref, sems.at[2 * groups])
    query_load.start()
    for copy in small:
        copy.wait()

    wide = (channels, channels * modes)
    spread = (iota(wide, 1) // modes == iota(wide, 0)).astype(BF16)
    chosen = (iota((filters, channels), 0) == index_ref[...]).astype(BF16)
    chosen = lax.dot_general(chosen, spread, NN, preferred_element_type=F32)
    own_mode = iota((modes, channels * modes), 1) % modes == iota((modes, channels * modes), 0)

    def lanes_of(table):
        spread_table = lax.dot_general(
            table, chosen, NN, precision=lax.Precision.HIGHEST, preferred_element_type=F32
        )
        return jnp.sum(jnp.where(own_mode, spread_table, 0.0), axis=0, keepdims=True)

    rate_row = lanes_of(rates_ref[...])
    gain_row = lanes_of(residues_ref[...]) * jnp.sqrt(one_minus_exp(2.0 * rate_row))
    own = iota((HALF, BLOCK), 1) // modes == iota((HALF, BLOCK), 0)
    place = lax.axis_index("ctx") % side
    odd, upper = place % 2 == 1, place >= 2
    same = iota((channels, channels), 0) == iota((channels, channels), 1)
    skip = jnp.sum(jnp.where(same, skip_row[...], 0.0), axis=1, keepdims=True)
    skip_ref[...] = jnp.broadcast_to(skip, skip_ref.shape)
    for g in range(groups):
        lanes = slice(g * BLOCK, (g + 1) * BLOCK)
        rate = rate_row[:, lanes]
        here = slice(g, g + 1)
        rate_ref[here, :] = rate
        gain_ref[here, :] = gain_row[:, lanes]
        passed = -rate * float(length)
        far_ref[0, here, :] = jnp.exp(passed * float(side))
        far_ref[1, here, :] = jnp.exp(passed * place.astype(F32))
        once, twice = jnp.exp(passed), jnp.exp(2.0 * passed)
        pair_ref[0, here, :] = jnp.where(odd, 1.0, once)
        pair_ref[1, here, :] = jnp.where(odd, once, 1.0)
        pair_ref[2, here, :] = jnp.where(odd, jnp.ones_like(once), 0.0)
        row_ref[0, here, :] = jnp.where(upper, 1.0, twice)
        row_ref[1, here, :] = jnp.where(upper, twice, 1.0)
        row_ref[2, here, :] = jnp.where(upper, jnp.where(odd, once, 1.0), 0.0)
        to_end = (BLOCK - 1 - iota((BLOCK, BLOCK), 0)).astype(F32)
        fade_high, fade_low = split(jnp.exp(-rate * to_end))
        fades = jnp.concatenate([fade_high, fade_high, fade_low], axis=0)
        later = (BLOCK * (blocks - 1 - iota((blocks, BLOCK), 0))).astype(F32)
        block_fade = jnp.exp(-rate * later)
        rows = slice(g * HALF, (g + 1) * HALF)
        total = jnp.zeros((HALF, BLOCK), F32)
        for copy in loads[g]:
            copy.wait()
        for start in range(0, blocks, 16):
            mixed = jnp.concatenate(
                [
                    key_ref[rows, b * BLOCK : (b + 1) * BLOCK] * value_ref[rows, b * BLOCK : (b + 1) * BLOCK]
                    for b in range(start, start + 16)
                ],
                axis=0,
            )
            mixed_ref[g, start * HALF : (start + 16) * HALF, :] = mixed
            high, low = split(mixed)
            states = lax.dot_general(
                jnp.concatenate([high, low, high], axis=1), fades, NN, preferred_element_type=F32
            )
            state_ref[g, start * HALF : (start + 16) * HALF, :] = states
            for b in range(16):
                total = total + block_fade[start + b : start + b + 1, :] * states[b * HALF : (b + 1) * HALF, :]
        end_ref[here, :] = jnp.sum(jnp.where(own, total, 0.0), axis=0, keepdims=True)
    query_load.wait()


def local_kernel(g, modes, mixed_ref, state_ref, skip_ref, rate_ref, gain_ref, base_ref, enter_ref, conv_rows):
    blocks = base_ref.shape[0] // HALF
    square = (BLOCK, BLOCK)
    own = iota((HALF, BLOCK), 1) // modes == iota((HALF, BLOCK), 0)
    causal = iota(square, 1) >= iota(square, 0)
    rate, gain = rate_ref[g : g + 1, :], gain_ref[g : g + 1, :]
    tail = gain * jnp.exp(-rate * iota(square, 0).astype(F32))
    taps = lax.dot_general(
        own.astype(F32), tail, NT, precision=lax.Precision.HIGHEST, preferred_element_type=F32
    )
    step = jnp.exp(-rate * float(BLOCK))
    state = jnp.zeros((HALF, BLOCK), F32)
    for b in range(blocks):
        some = slice(b * HALF, (b + 1) * HALF)
        enter_ref[some, :] = jnp.where(own, state, 0.0)
        state = state * step + state_ref[g, some, :]
    for c in range(HALF):
        shifted = pltpu.roll(jnp.broadcast_to(taps[c : c + 1, :], square), 0, 1, stride=1, stride_axis=0)
        weights = jnp.concatenate(split(jnp.where(causal, shifted, 0.0)), axis=1)
        signal = jnp.concatenate(split(mixed_ref[g, pl.ds(c, blocks, stride=HALF), :]), axis=0)
        parts = lax.dot_general(signal, weights, NN, preferred_element_type=F32)
        conv_rows[pl.ds(c, blocks, stride=HALF), :] = parts[:blocks, :BLOCK] + (
            parts[:blocks, BLOCK:] + parts[blocks:, :BLOCK]
        )
    skip = skip_ref[g * HALF : (g + 1) * HALF, :]
    for b in range(blocks):
        some = slice(b * HALF, (b + 1) * HALF)
        base_ref[some, :] = conv_rows[some, :] + skip * mixed_ref[g, some, :]


def output_kernel(
    modes, query_ref, rate_ref, gain_ref, far_ref, near_ref, carried_ref, *rest
):
    groups = rate_ref.shape[0]
    bases, enters = rest[:groups], rest[groups : 2 * groups]
    out_hbm, out_ref, sems = rest[2 * groups :]
    channels, length = query_ref.shape
    blocks = length // BLOCK
    own = iota((HALF, BLOCK), 1) // modes == iota((HALF, BLOCK), 0)
    square = (BLOCK, BLOCK)
    stores = []
    for g in range(groups):
        rows = slice(g * HALF, (g + 1) * HALF)
        here = slice(g, g + 1)
        rate, gain = rate_ref[here, :], gain_ref[here, :]
        after = iota(square, 0).astype(F32) + 1.0
        lead_high, lead_low = split(gain * jnp.exp(-rate * after))
        leads = jnp.concatenate([lead_high, lead_high, lead_low], axis=1)
        entered = near_ref[here, :] + far_ref[1, here, :] * carried_ref[here, :]
        fades = entered * jnp.exp(-rate * (BLOCK * iota((blocks, BLOCK), 0)).astype(F32))
        for start in range(0, blocks, 16):
            some = slice(start * HALF, (start + 16) * HALF)
            added = jnp.concatenate(
                [jnp.where(own, fades[b : b + 1, :], 0.0) for b in range(start, start + 16)], axis=0
            )
            high, low = split(enters[g][some, :] + added)
            conv = bases[g][some, :] + lax.dot_general(
                jnp.concatenate([high, low, high], axis=1), leads, NT, preferred_element_type=F32
            )
            for b in range(16):
                lanes = slice((start + b) * BLOCK, (start + b + 1) * BLOCK)
                out_ref[rows, lanes] = query_ref[rows, lanes] * conv[b * HALF : (b + 1) * HALF, :]
            lanes = slice(start * BLOCK, (start + 16) * BLOCK)
            store = pltpu.make_async_copy(out_ref.at[rows, lanes], out_hbm.at[rows, lanes], sems.at[len(stores)])
            store.start()
            stores.append(store)
    for store in stores:
        store.wait()


VMEM = pl.BlockSpec(memory_space=pltpu.VMEM)
HBM = pl.BlockSpec(memory_space=pltpu.HBM)
SIDE = 4


def shape(*dims):
    return jax.ShapeDtypeStruct(dims, F32)


def per_device(query_gate, key_gate, value_rows, filter_index, residues, decay_rates, skip_gain):
    channels, length = key_gate.shape
    modes = residues.shape[1]
    blocks = length // BLOCK
    groups = channels // HALF
    line = (groups, BLOCK)
    stripes = (groups, blocks * HALF, BLOCK)
    ends, rate, gain, far, pair, row, skip, mixed, state, query = pl.pallas_call(
        lambda *refs: state_kernel(SIDE, *refs),
        out_shape=(
            shape(*line), shape(*line), shape(*line), shape(2, *line), shape(3, *line), shape(3, *line),
            shape(channels, BLOCK), shape(*stripes), shape(*stripes), shape(channels, length),
        ),
        in_specs=[HBM] * 7,
        out_specs=(VMEM,) * 10,
        scratch_shapes=[
            pltpu.VMEM((1, channels), jnp.int32),
            pltpu.VMEM((modes, residues.shape[0]), F32),
            pltpu.VMEM((modes, residues.shape[0]), F32),
            pltpu.VMEM((1, channels), F32),
            pltpu.VMEM((channels, length), F32),
            pltpu.VMEM((channels, length), F32),
            pltpu.SemaphoreType.DMA((2 * groups + 5,)),
        ],
        compiler_params=pltpu.CompilerParams(vmem_limit_bytes=16 * 2**20),
        cost_estimate=pl.CostEstimate(flops=2 * 3 * 1024 * 128 * 128, bytes_accessed=2**20, transcendentals=2**16),
    )(
        *(
            pltpu.with_memory_space_constraint(array, pltpu.HBM)
            for array in (
                filter_index.reshape(1, channels), decay_rates.T, residues.T, skip_gain.reshape(1, channels),
                key_gate, value_rows, query_gate,
            )
        )
    )

    def local(g):
        return pl.pallas_call(
            lambda *refs: local_kernel(g, modes, *refs),
            out_shape=(shape(*stripes[1:]), shape(*stripes[1:])),
            in_specs=[VMEM] * 5,
            out_specs=(VMEM, VMEM),
            scratch_shapes=[pltpu.VMEM(stripes[1:], F32)],
            compiler_params=pltpu.CompilerParams(vmem_limit_bytes=16 * 2**20),
            cost_estimate=pl.CostEstimate(flops=2 * 4 * 512 * 128 * 128, bytes_accessed=2**19, transcendentals=2**14),
        )(mixed, state, skip, rate, gain)

    devices = lax.axis_size("ctx")
    partner = lax.ppermute(ends, "ctx", [(d, d ^ 1) for d in range(devices)])
    partner, first = lax.optimization_barrier((partner, local(0)))
    both = pair[0] * ends + pair[1] * partner
    across = lax.ppermute(both, "ctx", [(d, d ^ 3) for d in range(devices)])
    across, second = lax.optimization_barrier((across, local(1)))
    total = row[0] * both + row[1] * across
    near = pair[2] * partner + row[2] * across
    carried = jnp.zeros(line, F32)
    for r in range(devices // SIDE - 1):
        sent = total + far[0] * carried if r else total
        pairs = [(r * SIDE + x, (r + 1) * SIDE + x) for x in range(SIDE)]
        carried = carried + lax.ppermute(sent, "ctx", pairs)

    return pl.pallas_call(
        lambda *refs: output_kernel(modes, *refs),
        out_shape=shape(channels, length),
        in_specs=[VMEM] * (6 + 2 * groups),
        out_specs=HBM,
        scratch_shapes=[pltpu.VMEM((channels, length), F32), pltpu.SemaphoreType.DMA((groups * blocks // 16,))],
        compiler_params=pltpu.CompilerParams(vmem_limit_bytes=16 * 2**20),
        cost_estimate=pl.CostEstimate(flops=2 * 3 * 1024 * 128 * 128, bytes_accessed=2**21, transcendentals=2**16),
    )(query, rate, gain, far, near, carried, first[0], second[0], first[1], second[1])


def solution(mesh):
    placed = (P("chan", "ctx"), P("chan", "ctx"), P("chan", "ctx"), P("chan"), P(), P(), P("chan"))
    return jax.shard_map(
        per_device, mesh=mesh, in_specs=placed, out_specs=P("chan", "ctx"), check_vma=False
    )
```

```python
import jax
import jax.numpy as jnp
from jax import lax
from jax.experimental import pallas as pl
from jax.experimental.pallas import tpu as pltpu
from jax.sharding import PartitionSpec as P

BLOCK = 128
HALF = 8
F32, BF16 = jnp.float32, jnp.bfloat16
NN = (((1,), (0,)), ((), ()))
NT = (((1,), (1,)), ((), ()))


def split(value):
    high = value.astype(BF16)
    return high, (value - high.astype(F32)).astype(BF16)


def iota(shape, dim):
    return lax.broadcasted_iota(jnp.int32, shape, dim)


def one_minus_exp(x):
    series = jnp.full_like(x, 1.0)
    for k in range(9, 1, -1):
        series = 1.0 - x * series * (1.0 / k)
    return jnp.where(x <= 0.25, x * series, 1.0 - jnp.exp(-x))


def state_kernel(
    side, index_hbm, rates_hbm, residues_hbm, skip_hbm, key_hbm, value_hbm, query_hbm,
    end_ref, rate_ref, gain_ref, far_ref, pair_ref, row_ref, skip_ref, mixed_ref, state_ref, query_ref,
    index_ref, rates_ref, residues_ref, skip_row, key_ref, value_ref, sems,
):
    channels, length = key_ref.shape
    modes, filters = rates_ref.shape
    blocks = length // BLOCK
    groups = channels // HALF
    small = [
        pltpu.make_async_copy(source, target, sems.at[2 * groups + 1 + i])
        for i, (source, target) in enumerate(
            ((index_hbm, index_ref), (rates_hbm, rates_ref), (residues_hbm, residues_ref), (skip_hbm, skip_row))
        )
    ]
    for copy in small:
        copy.start()
    loads = []
    for g in range(groups):
        rows = slice(g * HALF, (g + 1) * HALF)
        pair = [
            pltpu.make_async_copy(source.at[rows, :], target.at[rows, :], sems.at[2 * g + i])
            for i, (source, target) in enumerate(((key_hbm, key_ref), (value_hbm, value_ref)))
        ]
        for copy in pair:
            copy.start()
        loads.append(pair)
    query_load = pltpu.make_async_copy(query_hbm, query_ref, sems.at[2 * groups])
    query_load.start()
    for copy in small:
        copy.wait()

    wide = (channels, channels * modes)
    spread = (iota(wide, 1) // modes == iota(wide, 0)).astype(BF16)
    chosen = (iota((filters, channels), 0) == index_ref[...]).astype(BF16)
    chosen = lax.dot_general(chosen, spread, NN, preferred_element_type=F32)
    own_mode = iota((modes, channels * modes), 1) % modes == iota((modes, channels * modes), 0)

    def lanes_of(table):
        spread_table = lax.dot_general(
            table, chosen, NN, precision=lax.Precision.HIGHEST, preferred_element_type=F32
        )
        return jnp.sum(jnp.where(own_mode, spread_table, 0.0), axis=0, keepdims=True)

    rate_row = lanes_of(rates_ref[...])
    gain_row = lanes_of(residues_ref[...]) * jnp.sqrt(one_minus_exp(2.0 * rate_row))
    own = iota((HALF, BLOCK), 1) // modes == iota((HALF, BLOCK), 0)
    place = lax.axis_index("ctx") % side
    odd, upper = place % 2 == 1, place >= 2
    same = iota((channels, channels), 0) == iota((channels, channels), 1)
    skip = jnp.sum(jnp.where(same, skip_row[...], 0.0), axis=1, keepdims=True)
    skip_ref[...] = jnp.broadcast_to(skip, skip_ref.shape)
    for g in range(groups):
        lanes = slice(g * BLOCK, (g + 1) * BLOCK)
        rate = rate_row[:, lanes]
        here = slice(g, g + 1)
        rate_ref[here, :] = rate
        gain_ref[here, :] = gain_row[:, lanes]
        passed = -rate * float(length)
        far_ref[0, here, :] = jnp.exp(passed * float(side))
        far_ref[1, here, :] = jnp.exp(passed * place.astype(F32))
        once, twice = jnp.exp(passed), jnp.exp(2.0 * passed)
        pair_ref[0, here, :] = jnp.where(odd, 1.0, once)
        pair_ref[1, here, :] = jnp.where(odd, once, 1.0)
        pair_ref[2, here, :] = jnp.where(odd, jnp.ones_like(once), 0.0)
        row_ref[0, here, :] = jnp.where(upper, 1.0, twice)
        row_ref[1, here, :] = jnp.where(upper, twice, 1.0)
        row_ref[2, here, :] = jnp.where(upper, jnp.where(odd, once, 1.0), 0.0)
        to_end = (BLOCK - 1 - iota((BLOCK, BLOCK), 0)).astype(F32)
        fade_high, fade_low = split(jnp.exp(-rate * to_end))
        fades = jnp.concatenate([fade_high, fade_high, fade_low], axis=0)
        later = (BLOCK * (blocks - 1 - iota((blocks, BLOCK), 0))).astype(F32)
        block_fade = jnp.exp(-rate * later)
        rows = slice(g * HALF, (g + 1) * HALF)
        total = jnp.zeros((HALF, BLOCK), F32)
        for copy in loads[g]:
            copy.wait()
        for start in range(0, blocks, 16):
            mixed = jnp.concatenate(
                [
                    key_ref[rows, b * BLOCK : (b + 1) * BLOCK] * value_ref[rows, b * BLOCK : (b + 1) * BLOCK]
                    for b in range(start, start + 16)
                ],
                axis=0,
            )
            mixed_ref[g, start * HALF : (start + 16) * HALF, :] = mixed
            high, low = split(mixed)
            states = lax.dot_general(
                jnp.concatenate([high, low, high], axis=1), fades, NN, preferred_element_type=F32
            )
            state_ref[g, start * HALF : (start + 16) * HALF, :] = states
            for b in range(16):
                total = total + block_fade[start + b : start + b + 1, :] * states[b * HALF : (b + 1) * HALF, :]
        end_ref[here, :] = jnp.sum(jnp.where(own, total, 0.0), axis=0, keepdims=True)
    query_load.wait()


def local_kernel(g, modes, mixed_ref, state_ref, skip_ref, rate_ref, gain_ref, base_ref, enter_ref, conv_rows):
    blocks = base_ref.shape[0] // HALF
    square = (BLOCK, BLOCK)
    own = iota((HALF, BLOCK), 1) // modes == iota((HALF, BLOCK), 0)
    causal = iota(square, 1) >= iota(square, 0)
    rate, gain = rate_ref[g : g + 1, :], gain_ref[g : g + 1, :]
    tail = gain * jnp.exp(-rate * iota(square, 0).astype(F32))
    taps = lax.dot_general(
        own.astype(F32), tail, NT, precision=lax.Precision.HIGHEST, preferred_element_type=F32
    )
    step = jnp.exp(-rate * float(BLOCK))
    state = jnp.zeros((HALF, BLOCK), F32)
    for b in range(blocks):
        some = slice(b * HALF, (b + 1) * HALF)
        enter_ref[some, :] = jnp.where(own, state, 0.0)
        state = state * step + state_ref[g, some, :]
    for c in range(HALF):
        shifted = pltpu.roll(jnp.broadcast_to(taps[c : c + 1, :], square), 0, 1, stride=1, stride_axis=0)
        weights = jnp.concatenate(split(jnp.where(causal, shifted, 0.0)), axis=1)
        signal = jnp.concatenate(split(mixed_ref[g, pl.ds(c, blocks, stride=HALF), :]), axis=0)
        parts = lax.dot_general(signal, weights, NN, preferred_element_type=F32)
        conv_rows[pl.ds(c, blocks, stride=HALF), :] = parts[:blocks, :BLOCK] + (
            parts[:blocks, BLOCK:] + parts[blocks:, :BLOCK]
        )
    skip = skip_ref[g * HALF : (g + 1) * HALF, :]
    for b in range(blocks):
        some = slice(b * HALF, (b + 1) * HALF)
        base_ref[some, :] = conv_rows[some, :] + skip * mixed_ref[g, some, :]


def output_kernel(
    modes, query_ref, rate_ref, gain_ref, far_ref, near_ref, carried_ref, *rest
):
    groups = rate_ref.shape[0]
    bases, enters = rest[:groups], rest[groups : 2 * groups]
    out_hbm, out_ref, sems = rest[2 * groups :]
    channels, length = query_ref.shape
    blocks = length // BLOCK
    own = iota((HALF, BLOCK), 1) // modes == iota((HALF, BLOCK), 0)
    square = (BLOCK, BLOCK)
    stores = []
    for g in range(groups):
        rows = slice(g * HALF, (g + 1) * HALF)
        here = slice(g, g + 1)
        rate, gain = rate_ref[here, :], gain_ref[here, :]
        after = iota(square, 0).astype(F32) + 1.0
        lead_high, lead_low = split(gain * jnp.exp(-rate * after))
        leads = jnp.concatenate([lead_high, lead_high, lead_low], axis=1)
        entered = near_ref[here, :] + far_ref[1, here, :] * carried_ref[here, :]
        fades = entered * jnp.exp(-rate * (BLOCK * iota((blocks, BLOCK), 0)).astype(F32))
        for start in range(0, blocks, 16):
            some = slice(start * HALF, (start + 16) * HALF)
            added = jnp.concatenate(
                [jnp.where(own, fades[b : b + 1, :], 0.0) for b in range(start, start + 16)], axis=0
            )
            high, low = split(enters[g][some, :] + added)
            conv = bases[g][some, :] + lax.dot_general(
                jnp.concatenate([high, low, high], axis=1), leads, NT, preferred_element_type=F32
            )
            for b in range(16):
                lanes = slice((start + b) * BLOCK, (start + b + 1) * BLOCK)
                out_ref[rows, lanes] = query_ref[rows, lanes] * conv[b * HALF : (b + 1) * HALF, :]
            lanes = slice(start * BLOCK, (start + 16) * BLOCK)
            store = pltpu.make_async_copy(out_ref.at[rows, lanes], out_hbm.at[rows, lanes], sems.at[len(stores)])
            store.start()
            stores.append(store)
    for store in stores:
        store.wait()


VMEM = pl.BlockSpec(memory_space=pltpu.VMEM)
HBM = pl.BlockSpec(memory_space=pltpu.HBM)
SIDE = 4


def shape(*dims):
    return jax.ShapeDtypeStruct(dims, F32)


def per_device(query_gate, key_gate, value_rows, filter_index, residues, decay_rates, skip_gain):
    channels, length = key_gate.shape
    modes = residues.shape[1]
    blocks = length // BLOCK
    groups = channels // HALF
    line = (groups, BLOCK)
    stripes = (groups, blocks * HALF, BLOCK)
    ends, rate, gain, far, pair, row, skip, mixed, state, query = pl.pallas_call(
        lambda *refs: state_kernel(SIDE, *refs),
        out_shape=(
            shape(*line), shape(*line), shape(*line), shape(2, *line), shape(3, *line), shape(3, *line),
            shape(channels, BLOCK), shape(*stripes), shape(*stripes), shape(channels, length),
        ),
        in_specs=[HBM] * 7,
        out_specs=(VMEM,) * 10,
        scratch_shapes=[
            pltpu.VMEM((1, channels), jnp.int32),
            pltpu.VMEM((modes, residues.shape[0]), F32),
            pltpu.VMEM((modes, residues.shape[0]), F32),
            pltpu.VMEM((1, channels), F32),
            pltpu.VMEM((channels, length), F32),
            pltpu.VMEM((channels, length), F32),
            pltpu.SemaphoreType.DMA((2 * groups + 5,)),
        ],
        compiler_params=pltpu.CompilerParams(vmem_limit_bytes=16 * 2**20),
        cost_estimate=pl.CostEstimate(flops=2 * 3 * 1024 * 128 * 128, bytes_accessed=2**20, transcendentals=2**16),
    )(
        *(
            pltpu.with_memory_space_constraint(array, pltpu.HBM)
            for array in (
                filter_index.reshape(1, channels), decay_rates.T, residues.T, skip_gain.reshape(1, channels),
                key_gate, value_rows, query_gate,
            )
        )
    )

    def local(g):
        return pl.pallas_call(
            lambda *refs: local_kernel(g, modes, *refs),
            out_shape=(shape(*stripes[1:]), shape(*stripes[1:])),
            in_specs=[VMEM] * 5,
            out_specs=(VMEM, VMEM),
            scratch_shapes=[pltpu.VMEM(stripes[1:], F32)],
            compiler_params=pltpu.CompilerParams(vmem_limit_bytes=16 * 2**20),
            cost_estimate=pl.CostEstimate(flops=2 * 4 * 512 * 128 * 128, bytes_accessed=2**19, transcendentals=2**14),
        )(mixed, state, skip, rate, gain)

    rows = lax.axis_size("ctx") // SIDE
    carried, near, mine = jnp.zeros(line, F32), jnp.zeros(line, F32), ends
    for r in range(rows):
        cells = [(r * SIDE + x, r * SIDE) for x in range(SIDE)]
        last = r == rows - 1
        partner = lax.ppermute(mine, "ctx", [(d, base + ((d - base) ^ 1)) for d, base in cells])
        if last:
            partner, first = lax.optimization_barrier((partner, local(0)))
        both = pair[0] * mine + pair[1] * partner
        across = lax.ppermute(both, "ctx", [(d, base + ((d - base) ^ 3)) for d, base in cells])
        if last:
            across, second = lax.optimization_barrier((across, local(1)))
        near = near + pair[2] * partner + row[2] * across
        if not last:
            sent = row[0] * both + row[1] * across + far[0] * carried
            sent, mine = lax.optimization_barrier((sent, mine))
            carried = carried + lax.ppermute(sent, "ctx", [(d, d + SIDE) for d, _ in cells])

    return pl.pallas_call(
        lambda *refs: output_kernel(modes, *refs),
        out_shape=shape(channels, length),
        in_specs=[VMEM] * (6 + 2 * groups),
        out_specs=HBM,
        scratch_shapes=[pltpu.VMEM((channels, length), F32), pltpu.SemaphoreType.DMA((groups * blocks // 16,))],
        compiler_params=pltpu.CompilerParams(vmem_limit_bytes=16 * 2**20),
        cost_estimate=pl.CostEstimate(flops=2 * 3 * 1024 * 128 * 128, bytes_accessed=2**21, transcendentals=2**16),
    )(query, rate, gain, far, near, carried, first[0], second[0], first[1], second[1])


def solution(mesh):
    placed = (P("chan", "ctx"), P("chan", "ctx"), P("chan", "ctx"), P("chan"), P(), P(), P("chan"))
    return jax.shard_map(
        per_device, mesh=mesh, in_specs=placed, out_specs=P("chan", "ctx"), check_vma=False
    )
```

```python
import jax
import jax.numpy as jnp
from jax import lax
from jax.experimental import pallas as pl
from jax.experimental.pallas import tpu as pltpu
from jax.sharding import PartitionSpec as P

BLOCK = 128
HALF = 8
F32, BF16 = jnp.float32, jnp.bfloat16
NN = (((1,), (0,)), ((), ()))
NT = (((1,), (1,)), ((), ()))


def split(value):
    high = value.astype(BF16)
    return high, (value - high.astype(F32)).astype(BF16)


def iota(shape, dim):
    return lax.broadcasted_iota(jnp.int32, shape, dim)


def one_minus_exp(x):
    series = jnp.full_like(x, 1.0)
    for k in range(9, 1, -1):
        series = 1.0 - x * series * (1.0 / k)
    return jnp.where(x <= 0.25, x * series, 1.0 - jnp.exp(-x))


def state_kernel(
    side, index_hbm, rates_hbm, residues_hbm, skip_hbm, key_hbm, value_hbm, query_hbm,
    end_ref, rate_ref, gain_ref, far_ref, pair_ref, row_ref, turn_ref, skip_ref, mixed_ref, state_ref, query_ref,
    index_ref, rates_ref, residues_ref, skip_row, key_ref, value_ref, sems,
):
    channels, length = key_ref.shape
    modes, filters = rates_ref.shape
    blocks = length // BLOCK
    groups = channels // HALF
    small = [
        pltpu.make_async_copy(source, target, sems.at[2 * groups + 1 + i])
        for i, (source, target) in enumerate(
            ((index_hbm, index_ref), (rates_hbm, rates_ref), (residues_hbm, residues_ref), (skip_hbm, skip_row))
        )
    ]
    for copy in small:
        copy.start()
    loads = []
    for g in range(groups):
        rows = slice(g * HALF, (g + 1) * HALF)
        pair = [
            pltpu.make_async_copy(source.at[rows, :], target.at[rows, :], sems.at[2 * g + i])
            for i, (source, target) in enumerate(((key_hbm, key_ref), (value_hbm, value_ref)))
        ]
        for copy in pair:
            copy.start()
        loads.append(pair)
    query_load = pltpu.make_async_copy(query_hbm, query_ref, sems.at[2 * groups])
    query_load.start()
    for copy in small:
        copy.wait()

    wide = (channels, channels * modes)
    spread = (iota(wide, 1) // modes == iota(wide, 0)).astype(BF16)
    chosen = (iota((filters, channels), 0) == index_ref[...]).astype(BF16)
    chosen = lax.dot_general(chosen, spread, NN, preferred_element_type=F32)
    own_mode = iota((modes, channels * modes), 1) % modes == iota((modes, channels * modes), 0)

    def lanes_of(table):
        spread_table = lax.dot_general(
            table, chosen, NN, precision=lax.Precision.HIGHEST, preferred_element_type=F32
        )
        return jnp.sum(jnp.where(own_mode, spread_table, 0.0), axis=0, keepdims=True)

    rate_row = lanes_of(rates_ref[...])
    gain_row = lanes_of(residues_ref[...]) * jnp.sqrt(one_minus_exp(2.0 * rate_row))
    own = iota((HALF, BLOCK), 1) // modes == iota((HALF, BLOCK), 0)
    place = lax.axis_index("ctx") % side
    first = lax.axis_index("ctx") < side
    odd, upper = place % 2 == 1, place >= 2
    same = iota((channels, channels), 0) == iota((channels, channels), 1)
    skip = jnp.sum(jnp.where(same, skip_row[...], 0.0), axis=1, keepdims=True)
    skip_ref[...] = jnp.broadcast_to(skip, skip_ref.shape)
    for g in range(groups):
        lanes = slice(g * BLOCK, (g + 1) * BLOCK)
        rate = rate_row[:, lanes]
        here = slice(g, g + 1)
        rate_ref[here, :] = rate
        gain_ref[here, :] = gain_row[:, lanes]
        passed = -rate * float(length)
        far_ref[0, here, :] = jnp.exp(passed * float(side))
        far_ref[1, here, :] = jnp.exp(passed * place.astype(F32))
        once, twice = jnp.exp(passed), jnp.exp(2.0 * passed)

        def to_side(k):
            ahead = side - 1 - (place - k + side) % side
            return jnp.exp(passed * ahead.astype(F32))

        pair_ref[0, here, :] = jnp.where(first, to_side(0), jnp.where(odd, 1.0, once))
        pair_ref[1, here, :] = jnp.where(first, to_side(1), jnp.where(odd, once, 1.0))
        pair_ref[2, here, :] = jnp.where((first & (place >= 1)) | odd, jnp.ones_like(once), 0.0)
        turn_ref[0, here, :] = to_side(2)
        turn_ref[1, here, :] = to_side(3)
        turn_ref[2, here, :] = jnp.where(place >= 2, once, 0.0)
        turn_ref[3, here, :] = jnp.where(place >= 3, twice, 0.0)
        row_ref[0, here, :] = jnp.where(upper, 1.0, twice)
        row_ref[1, here, :] = jnp.where(upper, twice, 1.0)
        row_ref[2, here, :] = jnp.where(upper, jnp.where(odd, once, 1.0), 0.0)
        to_end = (BLOCK - 1 - iota((BLOCK, BLOCK), 0)).astype(F32)
        fade_high, fade_low = split(jnp.exp(-rate * to_end))
        fades = jnp.concatenate([fade_high, fade_high, fade_low], axis=0)
        later = (BLOCK * (blocks - 1 - iota((blocks, BLOCK), 0))).astype(F32)
        block_fade = jnp.exp(-rate * later)
        rows = slice(g * HALF, (g + 1) * HALF)
        total = jnp.zeros((HALF, BLOCK), F32)
        for copy in loads[g]:
            copy.wait()
        for start in range(0, blocks, 16):
            mixed = jnp.concatenate(
                [
                    key_ref[rows, b * BLOCK : (b + 1) * BLOCK] * value_ref[rows, b * BLOCK : (b + 1) * BLOCK]
                    for b in range(start, start + 16)
                ],
                axis=0,
            )
            mixed_ref[g, start * HALF : (start + 16) * HALF, :] = mixed
            high, low = split(mixed)
            states = lax.dot_general(
                jnp.concatenate([high, low, high], axis=1), fades, NN, preferred_element_type=F32
            )
            state_ref[g, start * HALF : (start + 16) * HALF, :] = states
            for b in range(16):
                total = total + block_fade[start + b : start + b + 1, :] * states[b * HALF : (b + 1) * HALF, :]
        end_ref[here, :] = jnp.sum(jnp.where(own, total, 0.0), axis=0, keepdims=True)
    query_load.wait()


def local_kernel(g, modes, mixed_ref, state_ref, skip_ref, rate_ref, gain_ref, base_ref, enter_ref, conv_rows):
    blocks = base_ref.shape[0] // HALF
    square = (BLOCK, BLOCK)
    own = iota((HALF, BLOCK), 1) // modes == iota((HALF, BLOCK), 0)
    causal = iota(square, 1) >= iota(square, 0)
    rate, gain = rate_ref[g : g + 1, :], gain_ref[g : g + 1, :]
    tail = gain * jnp.exp(-rate * iota(square, 0).astype(F32))
    taps = lax.dot_general(
        own.astype(F32), tail, NT, precision=lax.Precision.HIGHEST, preferred_element_type=F32
    )
    step = jnp.exp(-rate * float(BLOCK))
    state = jnp.zeros((HALF, BLOCK), F32)
    for b in range(blocks):
        some = slice(b * HALF, (b + 1) * HALF)
        enter_ref[some, :] = jnp.where(own, state, 0.0)
        state = state * step + state_ref[g, some, :]
    for c in range(HALF):
        shifted = pltpu.roll(jnp.broadcast_to(taps[c : c + 1, :], square), 0, 1, stride=1, stride_axis=0)
        weights = jnp.concatenate(split(jnp.where(causal, shifted, 0.0)), axis=1)
        signal = jnp.concatenate(split(mixed_ref[g, pl.ds(c, blocks, stride=HALF), :]), axis=0)
        parts = lax.dot_general(signal, weights, NN, preferred_element_type=F32)
        conv_rows[pl.ds(c, blocks, stride=HALF), :] = parts[:blocks, :BLOCK] + (
            parts[:blocks, BLOCK:] + parts[blocks:, :BLOCK]
        )
    skip = skip_ref[g * HALF : (g + 1) * HALF, :]
    for b in range(blocks):
        some = slice(b * HALF, (b + 1) * HALF)
        base_ref[some, :] = conv_rows[some, :] + skip * mixed_ref[g, some, :]


def output_kernel(
    modes, query_ref, rate_ref, gain_ref, far_ref, near_ref, carried_ref, *rest
):
    groups = rate_ref.shape[0]
    bases, enters = rest[:groups], rest[groups : 2 * groups]
    out_hbm, out_ref, sems = rest[2 * groups :]
    channels, length = query_ref.shape
    blocks = length // BLOCK
    own = iota((HALF, BLOCK), 1) // modes == iota((HALF, BLOCK), 0)
    square = (BLOCK, BLOCK)
    stores = []
    for g in range(groups):
        rows = slice(g * HALF, (g + 1) * HALF)
        here = slice(g, g + 1)
        rate, gain = rate_ref[here, :], gain_ref[here, :]
        after = iota(square, 0).astype(F32) + 1.0
        lead_high, lead_low = split(gain * jnp.exp(-rate * after))
        leads = jnp.concatenate([lead_high, lead_high, lead_low], axis=1)
        entered = near_ref[here, :] + far_ref[1, here, :] * carried_ref[here, :]
        fades = entered * jnp.exp(-rate * (BLOCK * iota((blocks, BLOCK), 0)).astype(F32))
        for start in range(0, blocks, 16):
            some = slice(start * HALF, (start + 16) * HALF)
            added = jnp.concatenate(
                [jnp.where(own, fades[b : b + 1, :], 0.0) for b in range(start, start + 16)], axis=0
            )
            high, low = split(enters[g][some, :] + added)
            conv = bases[g][some, :] + lax.dot_general(
                jnp.concatenate([high, low, high], axis=1), leads, NT, preferred_element_type=F32
            )
            for b in range(16):
                lanes = slice((start + b) * BLOCK, (start + b + 1) * BLOCK)
                out_ref[rows, lanes] = query_ref[rows, lanes] * conv[b * HALF : (b + 1) * HALF, :]
            lanes = slice(start * BLOCK, (start + 16) * BLOCK)
            store = pltpu.make_async_copy(out_ref.at[rows, lanes], out_hbm.at[rows, lanes], sems.at[len(stores)])
            store.start()
            stores.append(store)
    for store in stores:
        store.wait()


VMEM = pl.BlockSpec(memory_space=pltpu.VMEM)
HBM = pl.BlockSpec(memory_space=pltpu.HBM)
SIDE = 4


def shape(*dims):
    return jax.ShapeDtypeStruct(dims, F32)


def per_device(query_gate, key_gate, value_rows, filter_index, residues, decay_rates, skip_gain):
    channels, length = key_gate.shape
    modes = residues.shape[1]
    blocks = length // BLOCK
    groups = channels // HALF
    line = (groups, BLOCK)
    stripes = (groups, blocks * HALF, BLOCK)
    ends, rate, gain, far, pair, row, turn, skip, mixed, state, query = pl.pallas_call(
        lambda *refs: state_kernel(SIDE, *refs),
        out_shape=(
            shape(*line), shape(*line), shape(*line), shape(2, *line), shape(3, *line), shape(3, *line), shape(4, *line),
            shape(channels, BLOCK), shape(*stripes), shape(*stripes), shape(channels, length),
        ),
        in_specs=[HBM] * 7,
        out_specs=(VMEM,) * 11,
        scratch_shapes=[
            pltpu.VMEM((1, channels), jnp.int32),
            pltpu.VMEM((modes, residues.shape[0]), F32),
            pltpu.VMEM((modes, residues.shape[0]), F32),
            pltpu.VMEM((1, channels), F32),
            pltpu.VMEM((channels, length), F32),
            pltpu.VMEM((channels, length), F32),
            pltpu.SemaphoreType.DMA((2 * groups + 5,)),
        ],
        compiler_params=pltpu.CompilerParams(vmem_limit_bytes=16 * 2**20),
        cost_estimate=pl.CostEstimate(flops=2 * 3 * 1024 * 128 * 128, bytes_accessed=2**20, transcendentals=2**16),
    )(
        *(
            pltpu.with_memory_space_constraint(array, pltpu.HBM)
            for array in (
                filter_index.reshape(1, channels), decay_rates.T, residues.T, skip_gain.reshape(1, channels),
                key_gate, value_rows, query_gate,
            )
        )
    )

    def local(g):
        return pl.pallas_call(
            lambda *refs: local_kernel(g, modes, *refs),
            out_shape=(shape(*stripes[1:]), shape(*stripes[1:])),
            in_specs=[VMEM] * 5,
            out_specs=(VMEM, VMEM),
            scratch_shapes=[pltpu.VMEM(stripes[1:], F32)],
            compiler_params=pltpu.CompilerParams(vmem_limit_bytes=16 * 2**20),
            cost_estimate=pl.CostEstimate(flops=2 * 4 * 512 * 128 * 128, bytes_accessed=2**19, transcendentals=2**14),
        )(mixed, state, skip, rate, gain)

    rows = lax.axis_size("ctx") // SIDE
    turns = [[(x, (x + k) % SIDE) for x in range(SIDE)] for k in range(SIDE)]
    met = [(d, d ^ 1) for d in range(SIDE, rows * SIDE)]
    partner = lax.ppermute(ends, "ctx", turns[1] + met)
    second = lax.ppermute(ends, "ctx", turns[2])
    third = lax.ppermute(ends, "ctx", turns[3])
    partner, local_first = lax.optimization_barrier((partner, local(0)))
    both = pair[0] * ends + pair[1] * partner
    near = pair[2] * partner + turn[2] * second + turn[3] * third
    sent = both + turn[0] * second + turn[1] * third
    carried = jnp.zeros(line, F32)
    for r in range(1, rows):
        sent, both = lax.optimization_barrier((sent, both))
        passed = lax.ppermute(sent, "ctx", [((r - 1) * SIDE + x, r * SIDE + x) for x in range(SIDE)])
        across = lax.ppermute(both, "ctx", [(r * SIDE + x, r * SIDE + (x ^ 3)) for x in range(SIDE)])
        if r == rows - 1:
            passed, local_second = lax.optimization_barrier((passed, local(1)))
        carried = carried + passed
        near = near + row[2] * across
        sent = row[0] * both + row[1] * across + far[0] * carried

    return pl.pallas_call(
        lambda *refs: output_kernel(modes, *refs),
        out_shape=shape(channels, length),
        in_specs=[VMEM] * (6 + 2 * groups),
        out_specs=HBM,
        scratch_shapes=[pltpu.VMEM((channels, length), F32), pltpu.SemaphoreType.DMA((groups * blocks // 16,))],
        compiler_params=pltpu.CompilerParams(vmem_limit_bytes=16 * 2**20),
        cost_estimate=pl.CostEstimate(flops=2 * 3 * 1024 * 128 * 128, bytes_accessed=2**21, transcendentals=2**16),
    )(query, rate, gain, far, near, carried, local_first[0], local_second[0], local_first[1], local_second[1])


def solution(mesh):
    placed = (P("chan", "ctx"), P("chan", "ctx"), P("chan", "ctx"), P("chan"), P(), P(), P("chan"))
    return jax.shard_map(
        per_device, mesh=mesh, in_specs=placed, out_specs=P("chan", "ctx"), check_vma=False
    )
```

```python
import jax
import jax.numpy as jnp
from jax import lax
from jax.experimental import pallas as pl
from jax.experimental.pallas import tpu as pltpu
from jax.sharding import PartitionSpec as P

BLOCK = 128
HALF = 8
F32, BF16 = jnp.float32, jnp.bfloat16
NN = (((1,), (0,)), ((), ()))
NT = (((1,), (1,)), ((), ()))


def split(value):
    high = value.astype(BF16)
    return high, (value - high.astype(F32)).astype(BF16)


def iota(shape, dim):
    return lax.broadcasted_iota(jnp.int32, shape, dim)


def one_minus_exp(x):
    series = jnp.full_like(x, 1.0)
    for k in range(9, 1, -1):
        series = 1.0 - x * series * (1.0 / k)
    return jnp.where(x <= 0.25, x * series, 1.0 - jnp.exp(-x))


def state_kernel(
    side, index_hbm, rates_hbm, residues_hbm, skip_hbm, key_hbm, value_hbm, query_hbm,
    end_ref, rate_ref, gain_ref, far_ref, row_ref, before_ref, skip_ref, mixed_ref, state_ref, query_ref,
    index_ref, rates_ref, residues_ref, skip_row, key_ref, value_ref, sems,
):
    channels, length = key_ref.shape
    modes, filters = rates_ref.shape
    blocks = length // BLOCK
    groups = channels // HALF
    small = [
        pltpu.make_async_copy(source, target, sems.at[2 * groups + 1 + i])
        for i, (source, target) in enumerate(
            ((index_hbm, index_ref), (rates_hbm, rates_ref), (residues_hbm, residues_ref), (skip_hbm, skip_row))
        )
    ]
    for copy in small:
        copy.start()
    loads = []
    for g in range(groups):
        rows = slice(g * HALF, (g + 1) * HALF)
        pair = [
            pltpu.make_async_copy(source.at[rows, :], target.at[rows, :], sems.at[2 * g + i])
            for i, (source, target) in enumerate(((key_hbm, key_ref), (value_hbm, value_ref)))
        ]
        for copy in pair:
            copy.start()
        loads.append(pair)
    query_load = pltpu.make_async_copy(query_hbm, query_ref, sems.at[2 * groups])
    query_load.start()
    for copy in small:
        copy.wait()

    wide = (channels, channels * modes)
    spread = (iota(wide, 1) // modes == iota(wide, 0)).astype(BF16)
    chosen = (iota((filters, channels), 0) == index_ref[...]).astype(BF16)
    chosen = lax.dot_general(chosen, spread, NN, preferred_element_type=F32)
    own_mode = iota((modes, channels * modes), 1) % modes == iota((modes, channels * modes), 0)

    def lanes_of(table):
        spread_table = lax.dot_general(
            table, chosen, NN, precision=lax.Precision.HIGHEST, preferred_element_type=F32
        )
        return jnp.sum(jnp.where(own_mode, spread_table, 0.0), axis=0, keepdims=True)

    rate_row = lanes_of(rates_ref[...])
    gain_row = lanes_of(residues_ref[...]) * jnp.sqrt(one_minus_exp(2.0 * rate_row))
    own = iota((HALF, BLOCK), 1) // modes == iota((HALF, BLOCK), 0)
    place = lax.axis_index("ctx") % side
    same = iota((channels, channels), 0) == iota((channels, channels), 1)
    skip = jnp.sum(jnp.where(same, skip_row[...], 0.0), axis=1, keepdims=True)
    skip_ref[...] = jnp.broadcast_to(skip, skip_ref.shape)
    for g in range(groups):
        lanes = slice(g * BLOCK, (g + 1) * BLOCK)
        rate = rate_row[:, lanes]
        here = slice(g, g + 1)
        rate_ref[here, :] = rate
        gain_ref[here, :] = gain_row[:, lanes]
        passed = -rate * float(length)
        far_ref[0, here, :] = jnp.exp(passed * float(side))
        far_ref[1, here, :] = jnp.exp(passed * place.astype(F32))
        for x in range(side):
            row_ref[x, here, :] = jnp.exp(passed * float(side - 1 - x))
            gap = (place - 1 - x).astype(F32)
            before_ref[x, here, :] = jnp.where(gap >= 0.0, jnp.exp(passed * jnp.maximum(gap, 0.0)), 0.0)
        to_end = (BLOCK - 1 - iota((BLOCK, BLOCK), 0)).astype(F32)
        fade_high, fade_low = split(jnp.exp(-rate * to_end))
        fades = jnp.concatenate([fade_high, fade_high, fade_low], axis=0)
        later = (BLOCK * (blocks - 1 - iota((blocks, BLOCK), 0))).astype(F32)
        block_fade = jnp.exp(-rate * later)
        rows = slice(g * HALF, (g + 1) * HALF)
        total = jnp.zeros((HALF, BLOCK), F32)
        for copy in loads[g]:
            copy.wait()
        for start in range(0, blocks, 16):
            mixed = jnp.concatenate(
                [
                    key_ref[rows, b * BLOCK : (b + 1) * BLOCK] * value_ref[rows, b * BLOCK : (b + 1) * BLOCK]
                    for b in range(start, start + 16)
                ],
                axis=0,
            )
            mixed_ref[g, start * HALF : (start + 16) * HALF, :] = mixed
            high, low = split(mixed)
            states = lax.dot_general(
                jnp.concatenate([high, low, high], axis=1), fades, NN, preferred_element_type=F32
            )
            state_ref[g, start * HALF : (start + 16) * HALF, :] = states
            for b in range(16):
                total = total + block_fade[start + b : start + b + 1, :] * states[b * HALF : (b + 1) * HALF, :]
        end_ref[here, :] = jnp.sum(jnp.where(own, total, 0.0), axis=0, keepdims=True)
    query_load.wait()


def local_kernel(g, modes, mixed_ref, state_ref, skip_ref, rate_ref, gain_ref, base_ref, enter_ref, conv_rows):
    blocks = base_ref.shape[0] // HALF
    square = (BLOCK, BLOCK)
    own = iota((HALF, BLOCK), 1) // modes == iota((HALF, BLOCK), 0)
    causal = iota(square, 1) >= iota(square, 0)
    rate, gain = rate_ref[g : g + 1, :], gain_ref[g : g + 1, :]
    tail = gain * jnp.exp(-rate * iota(square, 0).astype(F32))
    taps = lax.dot_general(
        own.astype(F32), tail, NT, precision=lax.Precision.HIGHEST, preferred_element_type=F32
    )
    step = jnp.exp(-rate * float(BLOCK))
    state = jnp.zeros((HALF, BLOCK), F32)
    for b in range(blocks):
        some = slice(b * HALF, (b + 1) * HALF)
        enter_ref[some, :] = jnp.where(own, state, 0.0)
        state = state * step + state_ref[g, some, :]
    for c in range(HALF):
        shifted = pltpu.roll(jnp.broadcast_to(taps[c : c + 1, :], square), 0, 1, stride=1, stride_axis=0)
        weights = jnp.concatenate(split(jnp.where(causal, shifted, 0.0)), axis=1)
        signal = jnp.concatenate(split(mixed_ref[g, pl.ds(c, blocks, stride=HALF), :]), axis=0)
        parts = lax.dot_general(signal, weights, NN, preferred_element_type=F32)
        conv_rows[pl.ds(c, blocks, stride=HALF), :] = parts[:blocks, :BLOCK] + (
            parts[:blocks, BLOCK:] + parts[blocks:, :BLOCK]
        )
    skip = skip_ref[g * HALF : (g + 1) * HALF, :]
    for b in range(blocks):
        some = slice(b * HALF, (b + 1) * HALF)
        base_ref[some, :] = conv_rows[some, :] + skip * mixed_ref[g, some, :]


def output_kernel(
    modes, query_ref, rate_ref, gain_ref, far_ref, near_ref, carried_ref, *rest
):
    groups = rate_ref.shape[0]
    bases, enters = rest[:groups], rest[groups : 2 * groups]
    out_hbm, out_ref, sems = rest[2 * groups :]
    channels, length = query_ref.shape
    blocks = length // BLOCK
    own = iota((HALF, BLOCK), 1) // modes == iota((HALF, BLOCK), 0)
    square = (BLOCK, BLOCK)
    stores = []
    for g in range(groups):
        rows = slice(g * HALF, (g + 1) * HALF)
        here = slice(g, g + 1)
        rate, gain = rate_ref[here, :], gain_ref[here, :]
        after = iota(square, 0).astype(F32) + 1.0
        lead_high, lead_low = split(gain * jnp.exp(-rate * after))
        leads = jnp.concatenate([lead_high, lead_high, lead_low], axis=1)
        entered = near_ref[here, :] + far_ref[1, here, :] * carried_ref[here, :]
        fades = entered * jnp.exp(-rate * (BLOCK * iota((blocks, BLOCK), 0)).astype(F32))
        for start in range(0, blocks, 16):
            some = slice(start * HALF, (start + 16) * HALF)
            added = jnp.concatenate(
                [jnp.where(own, fades[b : b + 1, :], 0.0) for b in range(start, start + 16)], axis=0
            )
            high, low = split(enters[g][some, :] + added)
            conv = bases[g][some, :] + lax.dot_general(
                jnp.concatenate([high, low, high], axis=1), leads, NT, preferred_element_type=F32
            )
            for b in range(16):
                lanes = slice((start + b) * BLOCK, (start + b + 1) * BLOCK)
                out_ref[rows, lanes] = query_ref[rows, lanes] * conv[b * HALF : (b + 1) * HALF, :]
            lanes = slice(start * BLOCK, (start + 16) * BLOCK)
            store = pltpu.make_async_copy(out_ref.at[rows, lanes], out_hbm.at[rows, lanes], sems.at[len(stores)])
            store.start()
            stores.append(store)
    for store in stores:
        store.wait()


VMEM = pl.BlockSpec(memory_space=pltpu.VMEM)
HBM = pl.BlockSpec(memory_space=pltpu.HBM)
SIDE = 4


def shape(*dims):
    return jax.ShapeDtypeStruct(dims, F32)


def per_device(query_gate, key_gate, value_rows, filter_index, residues, decay_rates, skip_gain):
    channels, length = key_gate.shape
    modes = residues.shape[1]
    blocks = length // BLOCK
    groups = channels // HALF
    line = (groups, BLOCK)
    stripes = (groups, blocks * HALF, BLOCK)
    ends, rate, gain, far, row, before, skip, mixed, state, query = pl.pallas_call(
        lambda *refs: state_kernel(SIDE, *refs),
        out_shape=(
            shape(*line), shape(*line), shape(*line), shape(2, *line), shape(SIDE, *line), shape(SIDE, *line),
            shape(channels, BLOCK), shape(*stripes), shape(*stripes), shape(channels, length),
        ),
        in_specs=[HBM] * 7,
        out_specs=(VMEM,) * 10,
        scratch_shapes=[
            pltpu.VMEM((1, channels), jnp.int32),
            pltpu.VMEM((modes, residues.shape[0]), F32),
            pltpu.VMEM((modes, residues.shape[0]), F32),
            pltpu.VMEM((1, channels), F32),
            pltpu.VMEM((channels, length), F32),
            pltpu.VMEM((channels, length), F32),
            pltpu.SemaphoreType.DMA((2 * groups + 5,)),
        ],
        compiler_params=pltpu.CompilerParams(vmem_limit_bytes=16 * 2**20),
        cost_estimate=pl.CostEstimate(flops=2 * 3 * 1024 * 128 * 128, bytes_accessed=2**20, transcendentals=2**16),
    )(
        *(
            pltpu.with_memory_space_constraint(array, pltpu.HBM)
            for array in (
                filter_index.reshape(1, channels), decay_rates.T, residues.T, skip_gain.reshape(1, channels),
                key_gate, value_rows, query_gate,
            )
        )
    )

    def local(g):
        return pl.pallas_call(
            lambda *refs: local_kernel(g, modes, *refs),
            out_shape=(shape(*stripes[1:]), shape(*stripes[1:])),
            in_specs=[VMEM] * 5,
            out_specs=(VMEM, VMEM),
            scratch_shapes=[pltpu.VMEM(stripes[1:], F32)],
            compiler_params=pltpu.CompilerParams(vmem_limit_bytes=16 * 2**20),
            cost_estimate=pl.CostEstimate(flops=2 * 4 * 512 * 128 * 128, bytes_accessed=2**19, transcendentals=2**14),
        )(mixed, state, skip, rate, gain)

    rows = lax.axis_size("ctx") // SIDE
    every = lax.all_gather(ends, "ctx", axis_index_groups=[[r * SIDE + x for x in range(SIDE)] for r in range(rows)])
    total = jnp.sum(row * every, axis=0)
    near = jnp.sum(before * every, axis=0)
    carried = jnp.zeros(line, F32)
    for r in range(1, rows):
        sent = total + far[0] * carried if r > 1 else total
        passed = lax.ppermute(sent, "ctx", [((r - 1) * SIDE + x, r * SIDE + x) for x in range(SIDE)])
        if r == rows - 1:
            passed, local_first, local_second = lax.optimization_barrier((passed, local(0), local(1)))
        carried = carried + passed

    return pl.pallas_call(
        lambda *refs: output_kernel(modes, *refs),
        out_shape=shape(channels, length),
        in_specs=[VMEM] * (6 + 2 * groups),
        out_specs=HBM,
        scratch_shapes=[pltpu.VMEM((channels, length), F32), pltpu.SemaphoreType.DMA((groups * blocks // 16,))],
        compiler_params=pltpu.CompilerParams(vmem_limit_bytes=16 * 2**20),
        cost_estimate=pl.CostEstimate(flops=2 * 3 * 1024 * 128 * 128, bytes_accessed=2**21, transcendentals=2**16),
    )(query, rate, gain, far, near, carried, local_first[0], local_second[0], local_first[1], local_second[1])


def solution(mesh):
    placed = (P("chan", "ctx"), P("chan", "ctx"), P("chan", "ctx"), P("chan"), P(), P(), P("chan"))
    return jax.shard_map(
        per_device, mesh=mesh, in_specs=placed, out_specs=P("chan", "ctx"), check_vma=False
    )
```

```python
import jax
import jax.numpy as jnp
from jax import lax
from jax.experimental import pallas as pl
from jax.experimental.pallas import tpu as pltpu
from jax.sharding import PartitionSpec as P

BLOCK = 128
HALF = 8
F32, BF16 = jnp.float32, jnp.bfloat16
NN = (((1,), (0,)), ((), ()))
NT = (((1,), (1,)), ((), ()))


def split(value):
    high = value.astype(BF16)
    return high, (value - high.astype(F32)).astype(BF16)


def iota(shape, dim):
    return lax.broadcasted_iota(jnp.int32, shape, dim)


def one_minus_exp(x):
    series = jnp.full_like(x, 1.0)
    for k in range(9, 1, -1):
        series = 1.0 - x * series * (1.0 / k)
    return jnp.where(x <= 0.25, x * series, 1.0 - jnp.exp(-x))


def state_kernel(
    side, index_hbm, rates_hbm, residues_hbm, skip_hbm, key_hbm, value_hbm, query_hbm,
    end_ref, rate_ref, gain_ref, far_ref, enter_ref, leave_ref, skip_ref, mixed_ref, state_ref, query_ref,
    index_ref, rates_ref, residues_ref, skip_row, key_ref, value_ref, sems,
):
    channels, length = key_ref.shape
    modes, filters = rates_ref.shape
    blocks = length // BLOCK
    groups = channels // HALF
    small = [
        pltpu.make_async_copy(source, target, sems.at[2 * groups + 1 + i])
        for i, (source, target) in enumerate(
            ((index_hbm, index_ref), (rates_hbm, rates_ref), (residues_hbm, residues_ref), (skip_hbm, skip_row))
        )
    ]
    for copy in small:
        copy.start()
    loads = []
    for g in range(groups):
        rows = slice(g * HALF, (g + 1) * HALF)
        pair = [
            pltpu.make_async_copy(source.at[rows, :], target.at[rows, :], sems.at[2 * g + i])
            for i, (source, target) in enumerate(((key_hbm, key_ref), (value_hbm, value_ref)))
        ]
        for copy in pair:
            copy.start()
        loads.append(pair)
    query_load = pltpu.make_async_copy(query_hbm, query_ref, sems.at[2 * groups])
    query_load.start()
    for copy in small:
        copy.wait()

    wide = (channels, channels * modes)
    spread = (iota(wide, 1) // modes == iota(wide, 0)).astype(BF16)
    chosen = (iota((filters, channels), 0) == index_ref[...]).astype(BF16)
    chosen = lax.dot_general(chosen, spread, NN, preferred_element_type=F32)
    own_mode = iota((modes, channels * modes), 1) % modes == iota((modes, channels * modes), 0)

    def lanes_of(table):
        spread_table = lax.dot_general(
            table, chosen, NN, precision=lax.Precision.HIGHEST, preferred_element_type=F32
        )
        return jnp.sum(jnp.where(own_mode, spread_table, 0.0), axis=0, keepdims=True)

    rate_row = lanes_of(rates_ref[...])
    gain_row = lanes_of(residues_ref[...]) * jnp.sqrt(one_minus_exp(2.0 * rate_row))
    own = iota((HALF, BLOCK), 1) // modes == iota((HALF, BLOCK), 0)
    me = lax.axis_index("ctx")
    place, inner = me % side, (me >= side) & (me < 3 * side)
    member = iota((2 * side, BLOCK), 0)
    member_row = jnp.where(inner, 1 + member // side, 3 * (member // side))
    source = member_row * side + member % side
    counted = (source < me) & (inner | (member_row == me // side))
    handed = inner & (member < side)
    same = iota((channels, channels), 0) == iota((channels, channels), 1)
    skip = jnp.sum(jnp.where(same, skip_row[...], 0.0), axis=1, keepdims=True)
    skip_ref[...] = jnp.broadcast_to(skip, skip_ref.shape)
    for g in range(groups):
        lanes = slice(g * BLOCK, (g + 1) * BLOCK)
        rate = rate_row[:, lanes]
        here = slice(g, g + 1)
        rate_ref[here, :] = rate
        gain_ref[here, :] = gain_row[:, lanes]
        passed = -rate * float(length)
        far_ref[here, :] = jnp.exp(passed * place.astype(F32))

        def faded(wanted, steps):
            return jnp.where(wanted, jnp.exp(passed * jnp.maximum(steps, 0).astype(F32)), 0.0)

        tables = (
            (enter_ref, 0, faded(counted, me - 1 - source)),
            (enter_ref, 1, faded(handed, me - 1 - member)),
            (leave_ref, 0, faded(member >= 0, 2 * side - 1 - member)),
            (leave_ref, 1, faded(member < side, 3 * side - 1 - member)),
        )
        for target, part, table in tables:
            for j in range(2 * side):
                target[j, part * groups + g : part * groups + g + 1, :] = table[j : j + 1, :]
        to_end = (BLOCK - 1 - iota((BLOCK, BLOCK), 0)).astype(F32)
        fade_high, fade_low = split(jnp.exp(-rate * to_end))
        fades = jnp.concatenate([fade_high, fade_high, fade_low], axis=0)
        later = (BLOCK * (blocks - 1 - iota((blocks, BLOCK), 0))).astype(F32)
        block_fade = jnp.exp(-rate * later)
        rows = slice(g * HALF, (g + 1) * HALF)
        total = jnp.zeros((HALF, BLOCK), F32)
        for copy in loads[g]:
            copy.wait()
        for start in range(0, blocks, 16):
            mixed = jnp.concatenate(
                [
                    key_ref[rows, b * BLOCK : (b + 1) * BLOCK] * value_ref[rows, b * BLOCK : (b + 1) * BLOCK]
                    for b in range(start, start + 16)
                ],
                axis=0,
            )
            mixed_ref[g, start * HALF : (start + 16) * HALF, :] = mixed
            high, low = split(mixed)
            states = lax.dot_general(
                jnp.concatenate([high, low, high], axis=1), fades, NN, preferred_element_type=F32
            )
            state_ref[g, start * HALF : (start + 16) * HALF, :] = states
            for b in range(16):
                total = total + block_fade[start + b : start + b + 1, :] * states[b * HALF : (b + 1) * HALF, :]
        end_ref[here, :] = jnp.sum(jnp.where(own, total, 0.0), axis=0, keepdims=True)
    query_load.wait()


def local_kernel(g, modes, mixed_ref, state_ref, skip_ref, rate_ref, gain_ref, base_ref, enter_ref, conv_rows):
    blocks = base_ref.shape[0] // HALF
    square = (BLOCK, BLOCK)
    own = iota((HALF, BLOCK), 1) // modes == iota((HALF, BLOCK), 0)
    causal = iota(square, 1) >= iota(square, 0)
    rate, gain = rate_ref[g : g + 1, :], gain_ref[g : g + 1, :]
    tail = gain * jnp.exp(-rate * iota(square, 0).astype(F32))
    taps = lax.dot_general(
        own.astype(F32), tail, NT, precision=lax.Precision.HIGHEST, preferred_element_type=F32
    )
    step = jnp.exp(-rate * float(BLOCK))
    state = jnp.zeros((HALF, BLOCK), F32)
    for b in range(blocks):
        some = slice(b * HALF, (b + 1) * HALF)
        enter_ref[some, :] = jnp.where(own, state, 0.0)
        state = state * step + state_ref[g, some, :]
    for c in range(HALF):
        shifted = pltpu.roll(jnp.broadcast_to(taps[c : c + 1, :], square), 0, 1, stride=1, stride_axis=0)
        weights = jnp.concatenate(split(jnp.where(causal, shifted, 0.0)), axis=1)
        signal = jnp.concatenate(split(mixed_ref[g, pl.ds(c, blocks, stride=HALF), :]), axis=0)
        parts = lax.dot_general(signal, weights, NN, preferred_element_type=F32)
        conv_rows[pl.ds(c, blocks, stride=HALF), :] = parts[:blocks, :BLOCK] + (
            parts[:blocks, BLOCK:] + parts[blocks:, :BLOCK]
        )
    skip = skip_ref[g * HALF : (g + 1) * HALF, :]
    for b in range(blocks):
        some = slice(b * HALF, (b + 1) * HALF)
        base_ref[some, :] = conv_rows[some, :] + skip * mixed_ref[g, some, :]


def output_kernel(
    modes, query_ref, rate_ref, gain_ref, far_ref, near_ref, carried_ref, *rest
):
    groups = rate_ref.shape[0]
    bases, enters = rest[:groups], rest[groups : 2 * groups]
    out_hbm, out_ref, sems = rest[2 * groups :]
    channels, length = query_ref.shape
    blocks = length // BLOCK
    own = iota((HALF, BLOCK), 1) // modes == iota((HALF, BLOCK), 0)
    square = (BLOCK, BLOCK)
    stores = []
    for g in range(groups):
        rows = slice(g * HALF, (g + 1) * HALF)
        here = slice(g, g + 1)
        rate, gain = rate_ref[here, :], gain_ref[here, :]
        after = iota(square, 0).astype(F32) + 1.0
        lead_high, lead_low = split(gain * jnp.exp(-rate * after))
        leads = jnp.concatenate([lead_high, lead_high, lead_low], axis=1)
        entered = near_ref[here, :] + far_ref[here, :] * carried_ref[here, :]
        fades = entered * jnp.exp(-rate * (BLOCK * iota((blocks, BLOCK), 0)).astype(F32))
        for start in range(0, blocks, 16):
            some = slice(start * HALF, (start + 16) * HALF)
            added = jnp.concatenate(
                [jnp.where(own, fades[b : b + 1, :], 0.0) for b in range(start, start + 16)], axis=0
            )
            high, low = split(enters[g][some, :] + added)
            conv = bases[g][some, :] + lax.dot_general(
                jnp.concatenate([high, low, high], axis=1), leads, NT, preferred_element_type=F32
            )
            for b in range(16):
                lanes = slice((start + b) * BLOCK, (start + b + 1) * BLOCK)
                out_ref[rows, lanes] = query_ref[rows, lanes] * conv[b * HALF : (b + 1) * HALF, :]
            lanes = slice(start * BLOCK, (start + 16) * BLOCK)
            store = pltpu.make_async_copy(out_ref.at[rows, lanes], out_hbm.at[rows, lanes], sems.at[len(stores)])
            store.start()
            stores.append(store)
    for store in stores:
        store.wait()


VMEM = pl.BlockSpec(memory_space=pltpu.VMEM)
HBM = pl.BlockSpec(memory_space=pltpu.HBM)
SIDE = 4


def shape(*dims):
    return jax.ShapeDtypeStruct(dims, F32)


def per_device(query_gate, key_gate, value_rows, filter_index, residues, decay_rates, skip_gain):
    channels, length = key_gate.shape
    modes = residues.shape[1]
    blocks = length // BLOCK
    groups = channels // HALF
    line = (groups, BLOCK)
    stripes = (groups, blocks * HALF, BLOCK)
    ends, rate, gain, far, enter, leave, skip, mixed, state, query = pl.pallas_call(
        lambda *refs: state_kernel(SIDE, *refs),
        out_shape=(
            shape(*line), shape(*line), shape(*line), shape(*line), shape(2 * SIDE, 2 * groups, BLOCK), shape(2 * SIDE, 2 * groups, BLOCK),
            shape(channels, BLOCK), shape(*stripes), shape(*stripes), shape(channels, length),
        ),
        in_specs=[HBM] * 7,
        out_specs=(VMEM,) * 10,
        scratch_shapes=[
            pltpu.VMEM((1, channels), jnp.int32),
            pltpu.VMEM((modes, residues.shape[0]), F32),
            pltpu.VMEM((modes, residues.shape[0]), F32),
            pltpu.VMEM((1, channels), F32),
            pltpu.VMEM((channels, length), F32),
            pltpu.VMEM((channels, length), F32),
            pltpu.SemaphoreType.DMA((2 * groups + 5,)),
        ],
        compiler_params=pltpu.CompilerParams(vmem_limit_bytes=16 * 2**20),
        cost_estimate=pl.CostEstimate(flops=2 * 3 * 1024 * 128 * 128, bytes_accessed=2**20, transcendentals=2**16),
    )(
        *(
            pltpu.with_memory_space_constraint(array, pltpu.HBM)
            for array in (
                filter_index.reshape(1, channels), decay_rates.T, residues.T, skip_gain.reshape(1, channels),
                key_gate, value_rows, query_gate,
            )
        )
    )

    def local(g):
        return pl.pallas_call(
            lambda *refs: local_kernel(g, modes, *refs),
            out_shape=(shape(*stripes[1:]), shape(*stripes[1:])),
            in_specs=[VMEM] * 5,
            out_specs=(VMEM, VMEM),
            scratch_shapes=[pltpu.VMEM(stripes[1:], F32)],
            compiler_params=pltpu.CompilerParams(vmem_limit_bytes=16 * 2**20),
            cost_estimate=pl.CostEstimate(flops=2 * 4 * 512 * 128 * 128, bytes_accessed=2**19, transcendentals=2**14),
        )(mixed, state, skip, rate, gain)

    handed = lax.ppermute(ends, "ctx", [(x, SIDE + x) for x in range(SIDE)])
    own = jnp.concatenate([ends, handed], axis=0).reshape(1, 1, -1)
    every = lax.all_to_all(
        jnp.broadcast_to(own, (2 * SIDE, 1, own.size)),
        "ctx",
        split_axis=0,
        concat_axis=0,
        tiled=True,
        axis_index_groups=[[*range(SIDE), *range(3 * SIDE, 4 * SIDE)], [*range(SIDE, 3 * SIDE)]],
    )
    every, local_first, local_second = lax.optimization_barrier((every, local(0), local(1)))
    every = every.reshape(2 * SIDE, 2 * groups, BLOCK)
    near = jnp.sum((enter * every).reshape(4 * SIDE, *line), axis=0)
    sent = jnp.sum((leave * every).reshape(4 * SIDE, *line), axis=0)
    carried = lax.ppermute(sent, "ctx", [(2 * SIDE + x, 3 * SIDE + x) for x in range(SIDE)])

    return pl.pallas_call(
        lambda *refs: output_kernel(modes, *refs),
        out_shape=shape(channels, length),
        in_specs=[VMEM] * (6 + 2 * groups),
        out_specs=HBM,
        scratch_shapes=[pltpu.VMEM((channels, length), F32), pltpu.SemaphoreType.DMA((groups * blocks // 16,))],
        compiler_params=pltpu.CompilerParams(vmem_limit_bytes=16 * 2**20),
        cost_estimate=pl.CostEstimate(flops=2 * 3 * 1024 * 128 * 128, bytes_accessed=2**21, transcendentals=2**16),
    )(query, rate, gain, far, near, carried, local_first[0], local_second[0], local_first[1], local_second[1])


def solution(mesh):
    placed = (P("chan", "ctx"), P("chan", "ctx"), P("chan", "ctx"), P("chan"), P(), P(), P("chan"))
    return jax.shard_map(
        per_device, mesh=mesh, in_specs=placed, out_specs=P("chan", "ctx"), check_vma=False
    )
```

```python
import jax
import jax.numpy as jnp
from jax import lax
from jax.experimental import pallas as pl
from jax.experimental.pallas import tpu as pltpu
from jax.sharding import PartitionSpec as P

BLOCK = 128
HALF = 8
F32, BF16 = jnp.float32, jnp.bfloat16
NN = (((1,), (0,)), ((), ()))
NT = (((1,), (1,)), ((), ()))


def split(value):
    high = value.astype(BF16)
    return high, (value - high.astype(F32)).astype(BF16)


def iota(shape, dim):
    return lax.broadcasted_iota(jnp.int32, shape, dim)


def one_minus_exp(x):
    series = jnp.full_like(x, 1.0)
    for k in range(9, 1, -1):
        series = 1.0 - x * series * (1.0 / k)
    return jnp.where(x <= 0.25, x * series, 1.0 - jnp.exp(-x))


def state_kernel(
    side, index_hbm, rates_hbm, residues_hbm, skip_hbm, key_hbm, value_hbm, query_hbm,
    end_ref, rate_ref, gain_ref, far_ref, enter_ref, leave_ref, skip_ref, mixed_ref, state_ref, query_ref,
    index_ref, rates_ref, residues_ref, skip_row, key_ref, value_ref, sems,
):
    channels, length = key_ref.shape
    modes, filters = rates_ref.shape
    blocks = length // BLOCK
    groups = channels // HALF
    small = [
        pltpu.make_async_copy(source, target, sems.at[2 * groups + 1 + i])
        for i, (source, target) in enumerate(
            ((index_hbm, index_ref), (rates_hbm, rates_ref), (residues_hbm, residues_ref), (skip_hbm, skip_row))
        )
    ]
    for copy in small:
        copy.start()
    loads = []
    for g in range(groups):
        rows = slice(g * HALF, (g + 1) * HALF)
        pair = [
            pltpu.make_async_copy(source.at[rows, :], target.at[rows, :], sems.at[2 * g + i])
            for i, (source, target) in enumerate(((key_hbm, key_ref), (value_hbm, value_ref)))
        ]
        for copy in pair:
            copy.start()
        loads.append(pair)
    query_load = pltpu.make_async_copy(query_hbm, query_ref, sems.at[2 * groups])
    query_load.start()
    for copy in small:
        copy.wait()

    wide = (channels, channels * modes)
    spread = (iota(wide, 1) // modes == iota(wide, 0)).astype(BF16)
    chosen = (iota((filters, channels), 0) == index_ref[...]).astype(BF16)
    chosen = lax.dot_general(chosen, spread, NN, preferred_element_type=F32)
    own_mode = iota((modes, channels * modes), 1) % modes == iota((modes, channels * modes), 0)

    def lanes_of(table):
        spread_table = lax.dot_general(
            table, chosen, NN, precision=lax.Precision.HIGHEST, preferred_element_type=F32
        )
        return jnp.sum(jnp.where(own_mode, spread_table, 0.0), axis=0, keepdims=True)

    rate_row = lanes_of(rates_ref[...])
    gain_row = lanes_of(residues_ref[...]) * jnp.sqrt(one_minus_exp(2.0 * rate_row))
    own = iota((HALF, BLOCK), 1) // modes == iota((HALF, BLOCK), 0)
    me = lax.axis_index("ctx")
    place, inner = me % side, (me >= side) & (me < 3 * side)
    member = iota((2 * side, BLOCK), 0)
    own_part = member // side == lax.axis_index("chan") % 2
    source = jnp.where(inner, side + member, me - place + member % side)
    counted = (source < me) & (inner | own_part)
    handed = inner & (member < side)
    same = iota((channels, channels), 0) == iota((channels, channels), 1)
    skip = jnp.sum(jnp.where(same, skip_row[...], 0.0), axis=1, keepdims=True)
    skip_ref[...] = jnp.broadcast_to(skip, skip_ref.shape)
    for g in range(groups):
        lanes = slice(g * BLOCK, (g + 1) * BLOCK)
        rate = rate_row[:, lanes]
        here = slice(g, g + 1)
        rate_ref[here, :] = rate
        gain_ref[here, :] = gain_row[:, lanes]
        passed = -rate * float(length)
        far_ref[here, :] = jnp.exp(passed * place.astype(F32))

        def faded(wanted, steps):
            return jnp.where(wanted, jnp.exp(passed * jnp.maximum(steps, 0).astype(F32)), 0.0)

        tables = (
            (enter_ref, 0, faded(counted, me - 1 - source)),
            (enter_ref, 1, faded(handed, me - 1 - member)),
            (leave_ref, 0, faded(member >= 0, 2 * side - 1 - member)),
            (leave_ref, 1, faded(member < side, 3 * side - 1 - member)),
        )
        for target, part, table in tables:
            for j in range(2 * side):
                target[j, part * groups + g : part * groups + g + 1, :] = table[j : j + 1, :]
        to_end = (BLOCK - 1 - iota((BLOCK, BLOCK), 0)).astype(F32)
        fade_high, fade_low = split(jnp.exp(-rate * to_end))
        fades = jnp.concatenate([fade_high, fade_high, fade_low], axis=0)
        later = (BLOCK * (blocks - 1 - iota((blocks, BLOCK), 0))).astype(F32)
        block_fade = jnp.exp(-rate * later)
        rows = slice(g * HALF, (g + 1) * HALF)
        total = jnp.zeros((HALF, BLOCK), F32)
        for copy in loads[g]:
            copy.wait()
        for start in range(0, blocks, 16):
            mixed = jnp.concatenate(
                [
                    key_ref[rows, b * BLOCK : (b + 1) * BLOCK] * value_ref[rows, b * BLOCK : (b + 1) * BLOCK]
                    for b in range(start, start + 16)
                ],
                axis=0,
            )
            mixed_ref[g, start * HALF : (start + 16) * HALF, :] = mixed
            high, low = split(mixed)
            states = lax.dot_general(
                jnp.concatenate([high, low, high], axis=1), fades, NN, preferred_element_type=F32
            )
            state_ref[g, start * HALF : (start + 16) * HALF, :] = states
            for b in range(16):
                total = total + block_fade[start + b : start + b + 1, :] * states[b * HALF : (b + 1) * HALF, :]
        end_ref[here, :] = jnp.sum(jnp.where(own, total, 0.0), axis=0, keepdims=True)
    query_load.wait()


def local_kernel(g, modes, mixed_ref, state_ref, skip_ref, rate_ref, gain_ref, base_ref, enter_ref, conv_rows):
    blocks = base_ref.shape[0] // HALF
    square = (BLOCK, BLOCK)
    own = iota((HALF, BLOCK), 1) // modes == iota((HALF, BLOCK), 0)
    causal = iota(square, 1) >= iota(square, 0)
    rate, gain = rate_ref[g : g + 1, :], gain_ref[g : g + 1, :]
    tail = gain * jnp.exp(-rate * iota(square, 0).astype(F32))
    taps = lax.dot_general(
        own.astype(F32), tail, NT, precision=lax.Precision.HIGHEST, preferred_element_type=F32
    )
    step = jnp.exp(-rate * float(BLOCK))
    state = jnp.zeros((HALF, BLOCK), F32)
    for b in range(blocks):
        some = slice(b * HALF, (b + 1) * HALF)
        enter_ref[some, :] = jnp.where(own, state, 0.0)
        state = state * step + state_ref[g, some, :]
    for c in range(HALF):
        shifted = pltpu.roll(jnp.broadcast_to(taps[c : c + 1, :], square), 0, 1, stride=1, stride_axis=0)
        weights = jnp.concatenate(split(jnp.where(causal, shifted, 0.0)), axis=1)
        signal = jnp.concatenate(split(mixed_ref[g, pl.ds(c, blocks, stride=HALF), :]), axis=0)
        parts = lax.dot_general(signal, weights, NN, preferred_element_type=F32)
        conv_rows[pl.ds(c, blocks, stride=HALF), :] = parts[:blocks, :BLOCK] + (
            parts[:blocks, BLOCK:] + parts[blocks:, :BLOCK]
        )
    skip = skip_ref[g * HALF : (g + 1) * HALF, :]
    for b in range(blocks):
        some = slice(b * HALF, (b + 1) * HALF)
        base_ref[some, :] = conv_rows[some, :] + skip * mixed_ref[g, some, :]


def output_kernel(
    modes, query_ref, rate_ref, gain_ref, far_ref, near_ref, carried_ref, *rest
):
    groups = rate_ref.shape[0]
    bases, enters = rest[:groups], rest[groups : 2 * groups]
    out_hbm, out_ref, sems = rest[2 * groups :]
    channels, length = query_ref.shape
    blocks = length // BLOCK
    own = iota((HALF, BLOCK), 1) // modes == iota((HALF, BLOCK), 0)
    square = (BLOCK, BLOCK)
    stores = []
    for g in range(groups):
        rows = slice(g * HALF, (g + 1) * HALF)
        here = slice(g, g + 1)
        rate, gain = rate_ref[here, :], gain_ref[here, :]
        after = iota(square, 0).astype(F32) + 1.0
        lead_high, lead_low = split(gain * jnp.exp(-rate * after))
        leads = jnp.concatenate([lead_high, lead_high, lead_low], axis=1)
        entered = near_ref[here, :] + far_ref[here, :] * carried_ref[here, :]
        fades = entered * jnp.exp(-rate * (BLOCK * iota((blocks, BLOCK), 0)).astype(F32))
        for start in range(0, blocks, 16):
            some = slice(start * HALF, (start + 16) * HALF)
            added = jnp.concatenate(
                [jnp.where(own, fades[b : b + 1, :], 0.0) for b in range(start, start + 16)], axis=0
            )
            high, low = split(enters[g][some, :] + added)
            conv = bases[g][some, :] + lax.dot_general(
                jnp.concatenate([high, low, high], axis=1), leads, NT, preferred_element_type=F32
            )
            for b in range(16):
                lanes = slice((start + b) * BLOCK, (start + b + 1) * BLOCK)
                out_ref[rows, lanes] = query_ref[rows, lanes] * conv[b * HALF : (b + 1) * HALF, :]
            lanes = slice(start * BLOCK, (start + 16) * BLOCK)
            store = pltpu.make_async_copy(out_ref.at[rows, lanes], out_hbm.at[rows, lanes], sems.at[len(stores)])
            store.start()
            stores.append(store)
    for store in stores:
        store.wait()


VMEM = pl.BlockSpec(memory_space=pltpu.VMEM)
HBM = pl.BlockSpec(memory_space=pltpu.HBM)
SIDE = 4


def shape(*dims):
    return jax.ShapeDtypeStruct(dims, F32)


def per_device(query_gate, key_gate, value_rows, filter_index, residues, decay_rates, skip_gain):
    channels, length = key_gate.shape
    modes = residues.shape[1]
    blocks = length // BLOCK
    groups = channels // HALF
    line = (groups, BLOCK)
    stripes = (groups, blocks * HALF, BLOCK)
    ends, rate, gain, far, enter, leave, skip, mixed, state, query = pl.pallas_call(
        lambda *refs: state_kernel(SIDE, *refs),
        out_shape=(
            shape(*line), shape(*line), shape(*line), shape(*line), shape(2 * SIDE, 2 * groups, BLOCK), shape(2 * SIDE, 2 * groups, BLOCK),
            shape(channels, BLOCK), shape(*stripes), shape(*stripes), shape(channels, length),
        ),
        in_specs=[HBM] * 7,
        out_specs=(VMEM,) * 10,
        scratch_shapes=[
            pltpu.VMEM((1, channels), jnp.int32),
            pltpu.VMEM((modes, residues.shape[0]), F32),
            pltpu.VMEM((modes, residues.shape[0]), F32),
            pltpu.VMEM((1, channels), F32),
            pltpu.VMEM((channels, length), F32),
            pltpu.VMEM((channels, length), F32),
            pltpu.SemaphoreType.DMA((2 * groups + 5,)),
        ],
        compiler_params=pltpu.CompilerParams(vmem_limit_bytes=16 * 2**20),
        cost_estimate=pl.CostEstimate(flops=2 * 3 * 1024 * 128 * 128, bytes_accessed=2**20, transcendentals=2**16),
    )(
        *(
            pltpu.with_memory_space_constraint(array, pltpu.HBM)
            for array in (
                filter_index.reshape(1, channels), decay_rates.T, residues.T, skip_gain.reshape(1, channels),
                key_gate, value_rows, query_gate,
            )
        )
    )

    def local(g):
        return pl.pallas_call(
            lambda *refs: local_kernel(g, modes, *refs),
            out_shape=(shape(*stripes[1:]), shape(*stripes[1:])),
            in_specs=[VMEM] * 5,
            out_specs=(VMEM, VMEM),
            scratch_shapes=[pltpu.VMEM(stripes[1:], F32)],
            compiler_params=pltpu.CompilerParams(vmem_limit_bytes=16 * 2**20),
            cost_estimate=pl.CostEstimate(flops=2 * 4 * 512 * 128 * 128, bytes_accessed=2**19, transcendentals=2**14),
        )(mixed, state, skip, rate, gain)

    parts = lax.axis_size("chan")
    inner = [[d * parts + part for d in range(SIDE, 3 * SIDE)] for part in range(parts)]
    outer = [
        [(row + x) * parts + pair + core for core in range(2) for x in range(SIDE)]
        for row in (0, 3 * SIDE)
        for pair in range(0, parts, 2)
    ]
    handed = lax.ppermute(ends, "ctx", [(x, SIDE + x) for x in range(SIDE)])
    own = jnp.concatenate([ends, handed], axis=0).reshape(1, 1, -1)
    every = lax.all_to_all(
        jnp.broadcast_to(own, (2 * SIDE, 1, own.size)),
        ("ctx", "chan"),
        split_axis=0,
        concat_axis=0,
        tiled=True,
        axis_index_groups=inner + outer,
    )
    every, local_first, local_second = lax.optimization_barrier((every, local(0), local(1)))
    every = every.reshape(2 * SIDE, 2 * groups, BLOCK)
    near = jnp.sum((enter * every).reshape(4 * SIDE, *line), axis=0)
    sent = jnp.sum((leave * every).reshape(4 * SIDE, *line), axis=0)
    carried = lax.ppermute(sent, "ctx", [(2 * SIDE + x, 3 * SIDE + x) for x in range(SIDE)])

    return pl.pallas_call(
        lambda *refs: output_kernel(modes, *refs),
        out_shape=shape(channels, length),
        in_specs=[VMEM] * (6 + 2 * groups),
        out_specs=HBM,
        scratch_shapes=[pltpu.VMEM((channels, length), F32), pltpu.SemaphoreType.DMA((groups * blocks // 16,))],
        compiler_params=pltpu.CompilerParams(vmem_limit_bytes=16 * 2**20),
        cost_estimate=pl.CostEstimate(flops=2 * 3 * 1024 * 128 * 128, bytes_accessed=2**21, transcendentals=2**16),
    )(query, rate, gain, far, near, carried, local_first[0], local_second[0], local_first[1], local_second[1])


def solution(mesh):
    placed = (P("chan", "ctx"), P("chan", "ctx"), P("chan", "ctx"), P("chan"), P(), P(), P("chan"))
    return jax.shard_map(
        per_device, mesh=mesh, in_specs=placed, out_specs=P("chan", "ctx"), check_vma=False
    )
```

```python
import jax
import jax.numpy as jnp
from jax import lax
from jax.experimental import pallas as pl
from jax.experimental.pallas import tpu as pltpu
from jax.sharding import PartitionSpec as P

BLOCK = 128
HALF = 8
F32, BF16 = jnp.float32, jnp.bfloat16
NN = (((1,), (0,)), ((), ()))
NT = (((1,), (1,)), ((), ()))


def split(value):
    high = value.astype(BF16)
    return high, (value - high.astype(F32)).astype(BF16)


def iota(shape, dim):
    return lax.broadcasted_iota(jnp.int32, shape, dim)


def one_minus_exp(x):
    series = jnp.full_like(x, 1.0)
    for k in range(9, 1, -1):
        series = 1.0 - x * series * (1.0 / k)
    return jnp.where(x <= 0.25, x * series, 1.0 - jnp.exp(-x))


def state_kernel(
    index_hbm, rates_hbm, residues_hbm, skip_hbm, key_hbm, value_hbm, query_hbm,
    end_ref, rate_ref, gain_ref, skip_ref, mixed_ref, state_ref, query_ref,
    index_ref, rates_ref, residues_ref, skip_row, key_ref, value_ref, sems,
):
    channels, length = key_ref.shape
    modes, filters = rates_ref.shape
    blocks = length // BLOCK
    groups = channels // HALF
    small = [
        pltpu.make_async_copy(source, target, sems.at[2 * groups + 1 + i])
        for i, (source, target) in enumerate(
            ((index_hbm, index_ref), (rates_hbm, rates_ref), (residues_hbm, residues_ref), (skip_hbm, skip_row))
        )
    ]
    for copy in small:
        copy.start()
    loads = []
    for g in range(groups):
        rows = slice(g * HALF, (g + 1) * HALF)
        pair = [
            pltpu.make_async_copy(source.at[rows, :], target.at[rows, :], sems.at[2 * g + i])
            for i, (source, target) in enumerate(((key_hbm, key_ref), (value_hbm, value_ref)))
        ]
        for copy in pair:
            copy.start()
        loads.append(pair)
    query_load = pltpu.make_async_copy(query_hbm, query_ref, sems.at[2 * groups])
    query_load.start()
    for copy in small + loads[0] + loads[1]:
        copy.wait()

    wide = (channels, channels * modes)
    spread = (iota(wide, 1) // modes == iota(wide, 0)).astype(BF16)
    chosen = (iota((filters, channels), 0) == index_ref[...]).astype(BF16)
    chosen = lax.dot_general(chosen, spread, NN, preferred_element_type=F32)
    own_mode = iota((modes, channels * modes), 1) % modes == iota((modes, channels * modes), 0)

    def lanes_of(table):
        spread_table = lax.dot_general(
            table, chosen, NN, precision=lax.Precision.HIGHEST, preferred_element_type=F32
        )
        return jnp.sum(jnp.where(own_mode, spread_table, 0.0), axis=0, keepdims=True)

    rate_row = lanes_of(rates_ref[...])
    gain_row = lanes_of(residues_ref[...]) * jnp.sqrt(one_minus_exp(2.0 * rate_row))
    own = iota((HALF, BLOCK), 1) // modes == iota((HALF, BLOCK), 0)
    same = iota((channels, channels), 0) == iota((channels, channels), 1)
    skip = jnp.sum(jnp.where(same, skip_row[...], 0.0), axis=1, keepdims=True)
    skip_ref[...] = jnp.broadcast_to(skip, skip_ref.shape)
    for g in range(groups):
        lanes = slice(g * BLOCK, (g + 1) * BLOCK)
        rate = rate_row[:, lanes]
        here = slice(g, g + 1)
        rate_ref[here, :] = rate
        gain_ref[here, :] = gain_row[:, lanes]
        to_end = (BLOCK - 1 - iota((BLOCK, BLOCK), 0)).astype(F32)
        fade_high, fade_low = split(jnp.exp(-rate * to_end))
        fades = jnp.concatenate([fade_high, fade_high, fade_low], axis=0)
        later = (BLOCK * (blocks - 1 - iota((blocks, BLOCK), 0))).astype(F32)
        block_fade = jnp.exp(-rate * later)
        rows = slice(g * HALF, (g + 1) * HALF)
        total = jnp.zeros((HALF, BLOCK), F32)
        for start in range(0, blocks, 16):
            mixed = jnp.concatenate(
                [
                    key_ref[rows, b * BLOCK : (b + 1) * BLOCK] * value_ref[rows, b * BLOCK : (b + 1) * BLOCK]
                    for b in range(start, start + 16)
                ],
                axis=0,
            )
            mixed_ref[g, start * HALF : (start + 16) * HALF, :] = mixed
            high, low = split(mixed)
            states = lax.dot_general(
                jnp.concatenate([high, low, high], axis=1), fades, NN, preferred_element_type=F32
            )
            state_ref[g, start * HALF : (start + 16) * HALF, :] = states
            for b in range(16):
                total = total + block_fade[start + b : start + b + 1, :] * states[b * HALF : (b + 1) * HALF, :]
        end_ref[here, :] = jnp.sum(jnp.where(own, total, 0.0), axis=0, keepdims=True)
    query_load.wait()


def weight_tables(side, length, rate_ref, far_ref, enter_ref, leave_ref):
    me = lax.axis_index("ctx")
    place, inner = me % side, (me >= side) & (me < 3 * side)
    member = iota((2 * side, BLOCK), 0)
    own_part = member // side == lax.axis_index("chan") % 2
    source = jnp.where(inner, side + member, me - place + member % side)
    counted = (source < me) & (inner | own_part)
    handed = inner & (member < side)
    groups = rate_ref.shape[0]
    for g in range(groups):
        here = slice(g, g + 1)
        rate = rate_ref[here, :]
        passed = -rate * float(length)
        far_ref[here, :] = jnp.exp(passed * place.astype(F32))

        def faded(wanted, steps):
            return jnp.where(wanted, jnp.exp(passed * jnp.maximum(steps, 0).astype(F32)), 0.0)

        tables = (
            (enter_ref, 0, faded(counted, me - 1 - source)),
            (enter_ref, 1, faded(handed, me - 1 - member)),
            (leave_ref, 0, faded(member >= 0, 2 * side - 1 - member)),
            (leave_ref, 1, faded(member < side, 3 * side - 1 - member)),
        )
        for target, part, table in tables:
            for j in range(2 * side):
                target[j, part * groups + g : part * groups + g + 1, :] = table[j : j + 1, :]


def local_kernel(g, modes, side, length, mixed_ref, state_ref, skip_ref, rate_ref, gain_ref, base_ref, enter_ref, *rest):
    conv_rows = rest[-1]
    if rest[:-1]:
        weight_tables(side, length, rate_ref, *rest[:-1])
    blocks = base_ref.shape[0] // HALF
    square = (BLOCK, BLOCK)
    own = iota((HALF, BLOCK), 1) // modes == iota((HALF, BLOCK), 0)
    causal = iota(square, 1) >= iota(square, 0)
    rate, gain = rate_ref[g : g + 1, :], gain_ref[g : g + 1, :]
    tail = gain * jnp.exp(-rate * iota(square, 0).astype(F32))
    taps = lax.dot_general(
        own.astype(F32), tail, NT, precision=lax.Precision.HIGHEST, preferred_element_type=F32
    )
    step = jnp.exp(-rate * float(BLOCK))
    state = jnp.zeros((HALF, BLOCK), F32)
    for b in range(blocks):
        some = slice(b * HALF, (b + 1) * HALF)
        enter_ref[some, :] = jnp.where(own, state, 0.0)
        state = state * step + state_ref[g, some, :]
    for c in range(HALF):
        shifted = pltpu.roll(jnp.broadcast_to(taps[c : c + 1, :], square), 0, 1, stride=1, stride_axis=0)
        weights = jnp.concatenate(split(jnp.where(causal, shifted, 0.0)), axis=1)
        signal = jnp.concatenate(split(mixed_ref[g, pl.ds(c, blocks, stride=HALF), :]), axis=0)
        parts = lax.dot_general(signal, weights, NN, preferred_element_type=F32)
        conv_rows[pl.ds(c, blocks, stride=HALF), :] = parts[:blocks, :BLOCK] + (
            parts[:blocks, BLOCK:] + parts[blocks:, :BLOCK]
        )
    skip = skip_ref[g * HALF : (g + 1) * HALF, :]
    for b in range(blocks):
        some = slice(b * HALF, (b + 1) * HALF)
        base_ref[some, :] = conv_rows[some, :] + skip * mixed_ref[g, some, :]


def output_kernel(
    modes, query_ref, rate_ref, gain_ref, far_ref, near_ref, carried_ref, *rest
):
    groups = rate_ref.shape[0]
    bases, enters = rest[:groups], rest[groups : 2 * groups]
    out_hbm, out_ref, sems = rest[2 * groups :]
    channels, length = query_ref.shape
    blocks = length // BLOCK
    own = iota((HALF, BLOCK), 1) // modes == iota((HALF, BLOCK), 0)
    square = (BLOCK, BLOCK)
    stores = []
    for g in range(groups):
        rows = slice(g * HALF, (g + 1) * HALF)
        here = slice(g, g + 1)
        rate, gain = rate_ref[here, :], gain_ref[here, :]
        after = iota(square, 0).astype(F32) + 1.0
        lead_high, lead_low = split(gain * jnp.exp(-rate * after))
        leads = jnp.concatenate([lead_high, lead_high, lead_low], axis=1)
        entered = near_ref[here, :] + far_ref[here, :] * carried_ref[here, :]
        fades = entered * jnp.exp(-rate * (BLOCK * iota((blocks, BLOCK), 0)).astype(F32))
        for start in range(0, blocks, 16):
            some = slice(start * HALF, (start + 16) * HALF)
            added = jnp.concatenate(
                [jnp.where(own, fades[b : b + 1, :], 0.0) for b in range(start, start + 16)], axis=0
            )
            high, low = split(enters[g][some, :] + added)
            conv = bases[g][some, :] + lax.dot_general(
                jnp.concatenate([high, low, high], axis=1), leads, NT, preferred_element_type=F32
            )
            for b in range(16):
                lanes = slice((start + b) * BLOCK, (start + b + 1) * BLOCK)
                out_ref[rows, lanes] = query_ref[rows, lanes] * conv[b * HALF : (b + 1) * HALF, :]
            lanes = slice(start * BLOCK, (start + 16) * BLOCK)
            store = pltpu.make_async_copy(out_ref.at[rows, lanes], out_hbm.at[rows, lanes], sems.at[len(stores)])
            store.start()
            stores.append(store)
    for store in stores:
        store.wait()


VMEM = pl.BlockSpec(memory_space=pltpu.VMEM)
HBM = pl.BlockSpec(memory_space=pltpu.HBM)
SIDE = 4


def shape(*dims):
    return jax.ShapeDtypeStruct(dims, F32)


def per_device(query_gate, key_gate, value_rows, filter_index, residues, decay_rates, skip_gain):
    channels, length = key_gate.shape
    modes = residues.shape[1]
    blocks = length // BLOCK
    groups = channels // HALF
    line = (groups, BLOCK)
    stripes = (groups, blocks * HALF, BLOCK)
    ends, rate, gain, skip, mixed, state, query = pl.pallas_call(
        state_kernel,
        out_shape=(
            shape(*line), shape(*line), shape(*line),
            shape(channels, BLOCK), shape(*stripes), shape(*stripes), shape(channels, length),
        ),
        in_specs=[HBM] * 7,
        out_specs=(VMEM,) * 7,
        scratch_shapes=[
            pltpu.VMEM((1, channels), jnp.int32),
            pltpu.VMEM((modes, residues.shape[0]), F32),
            pltpu.VMEM((modes, residues.shape[0]), F32),
            pltpu.VMEM((1, channels), F32),
            pltpu.VMEM((channels, length), F32),
            pltpu.VMEM((channels, length), F32),
            pltpu.SemaphoreType.DMA((2 * groups + 5,)),
        ],
        compiler_params=pltpu.CompilerParams(vmem_limit_bytes=16 * 2**20),
        cost_estimate=pl.CostEstimate(flops=2 * 3 * 1024 * 128 * 128, bytes_accessed=2**20, transcendentals=2**16),
    )(
        *(
            pltpu.with_memory_space_constraint(array, pltpu.HBM)
            for array in (
                filter_index.reshape(1, channels), decay_rates.T, residues.T, skip_gain.reshape(1, channels),
                key_gate, value_rows, query_gate,
            )
        )
    )

    tables = (shape(*line), shape(2 * SIDE, 2 * groups, BLOCK), shape(2 * SIDE, 2 * groups, BLOCK))

    def local(g, more=()):
        return pl.pallas_call(
            lambda *refs: local_kernel(g, modes, SIDE, length, *refs),
            out_shape=(shape(*stripes[1:]), shape(*stripes[1:]), *more),
            in_specs=[VMEM] * 5,
            out_specs=(VMEM,) * (2 + len(more)),
            scratch_shapes=[pltpu.VMEM(stripes[1:], F32)],
            compiler_params=pltpu.CompilerParams(vmem_limit_bytes=16 * 2**20),
            cost_estimate=pl.CostEstimate(flops=2 * 4 * 512 * 128 * 128, bytes_accessed=2**19, transcendentals=2**14),
        )(mixed, state, skip, rate, gain)

    parts = lax.axis_size("chan")
    inner = [[d * parts + part for d in range(SIDE, 3 * SIDE)] for part in range(parts)]
    outer = [
        [(row + x) * parts + pair + core for core in range(2) for x in range(SIDE)]
        for row in (0, 3 * SIDE)
        for pair in range(0, parts, 2)
    ]
    handed = lax.ppermute(ends, "ctx", [(x, SIDE + x) for x in range(SIDE)])
    handed, local_first, local_second = lax.optimization_barrier((handed, local(0, tables), local(1)))
    far, enter, leave = local_first[2:]
    own = jnp.concatenate([ends, handed], axis=0).reshape(1, 1, -1)
    every = lax.all_to_all(
        jnp.broadcast_to(own, (2 * SIDE, 1, own.size)),
        ("ctx", "chan"),
        split_axis=0,
        concat_axis=0,
        tiled=True,
        axis_index_groups=inner + outer,
    )
    every = every.reshape(2 * SIDE, 2 * groups, BLOCK)
    near = jnp.sum((enter * every).reshape(4 * SIDE, *line), axis=0)
    sent = jnp.sum((leave * every).reshape(4 * SIDE, *line), axis=0)
    carried = lax.ppermute(sent, "ctx", [(2 * SIDE + x, 3 * SIDE + x) for x in range(SIDE)])

    return pl.pallas_call(
        lambda *refs: output_kernel(modes, *refs),
        out_shape=shape(channels, length),
        in_specs=[VMEM] * (6 + 2 * groups),
        out_specs=HBM,
        scratch_shapes=[pltpu.VMEM((channels, length), F32), pltpu.SemaphoreType.DMA((groups * blocks // 16,))],
        compiler_params=pltpu.CompilerParams(vmem_limit_bytes=16 * 2**20),
        cost_estimate=pl.CostEstimate(flops=2 * 3 * 1024 * 128 * 128, bytes_accessed=2**21, transcendentals=2**16),
    )(query, rate, gain, far, near, carried, local_first[0], local_second[0], local_first[1], local_second[1])


def solution(mesh):
    placed = (P("chan", "ctx"), P("chan", "ctx"), P("chan", "ctx"), P("chan"), P(), P(), P("chan"))
    return jax.shard_map(
        per_device, mesh=mesh, in_specs=placed, out_specs=P("chan", "ctx"), check_vma=False
    )
```

```python
import jax
import jax.numpy as jnp
from jax import lax
from jax.experimental import pallas as pl
from jax.experimental.pallas import tpu as pltpu
from jax.sharding import PartitionSpec as P

BLOCK = 128
HALF = 8
F32, BF16 = jnp.float32, jnp.bfloat16
NN = (((1,), (0,)), ((), ()))
NT = (((1,), (1,)), ((), ()))


def split(value):
    high = value.astype(BF16)
    return high, (value - high.astype(F32)).astype(BF16)


def iota(shape, dim):
    return lax.broadcasted_iota(jnp.int32, shape, dim)


def one_minus_exp(x):
    series = jnp.full_like(x, 1.0)
    for k in range(9, 1, -1):
        series = 1.0 - x * series * (1.0 / k)
    return jnp.where(x <= 0.25, x * series, 1.0 - jnp.exp(-x))


def state_kernel(
    index_hbm, rates_hbm, residues_hbm, skip_hbm, key_hbm, value_hbm, query_hbm,
    end_ref, rate_ref, weight_ref, skip_ref, mixed_ref, state_ref, query_ref,
    index_ref, rates_ref, residues_ref, skip_row, key_ref, value_ref, sems,
):
    channels, length = key_ref.shape
    modes, filters = rates_ref.shape
    blocks = length // BLOCK
    groups = channels // HALF
    small = [
        pltpu.make_async_copy(source, target, sems.at[2 * groups + 1 + i])
        for i, (source, target) in enumerate(
            ((index_hbm, index_ref), (rates_hbm, rates_ref), (residues_hbm, residues_ref), (skip_hbm, skip_row))
        )
    ]
    for copy in small:
        copy.start()
    loads = []
    for g in range(groups):
        rows = slice(g * HALF, (g + 1) * HALF)
        pair = [
            pltpu.make_async_copy(source.at[rows, :], target.at[rows, :], sems.at[2 * g + i])
            for i, (source, target) in enumerate(((key_hbm, key_ref), (value_hbm, value_ref)))
        ]
        for copy in pair:
            copy.start()
        loads.append(pair)
    query_load = pltpu.make_async_copy(query_hbm, query_ref, sems.at[2 * groups])
    query_load.start()
    for copy in small:
        copy.wait()

    wide = (channels, channels * modes)
    spread = (iota(wide, 1) // modes == iota(wide, 0)).astype(BF16)
    chosen = (iota((filters, channels), 0) == index_ref[...]).astype(BF16)
    chosen = lax.dot_general(chosen, spread, NN, preferred_element_type=F32)
    own_mode = iota((modes, channels * modes), 1) % modes == iota((modes, channels * modes), 0)

    def lanes_of(table):
        spread_table = lax.dot_general(
            table, chosen, NN, precision=lax.Precision.HIGHEST, preferred_element_type=F32
        )
        return jnp.sum(jnp.where(own_mode, spread_table, 0.0), axis=0, keepdims=True)

    rate_row = lanes_of(rates_ref[...])
    weight_row = lanes_of(residues_ref[...])
    own = iota((HALF, BLOCK), 1) // modes == iota((HALF, BLOCK), 0)
    same = iota((channels, channels), 0) == iota((channels, channels), 1)
    skip = jnp.sum(jnp.where(same, skip_row[...], 0.0), axis=1, keepdims=True)
    skip_ref[...] = jnp.broadcast_to(skip, skip_ref.shape)
    for g in range(groups):
        lanes = slice(g * BLOCK, (g + 1) * BLOCK)
        rate = rate_row[:, lanes]
        here = slice(g, g + 1)
        rate_ref[here, :] = rate
        weight_ref[here, :] = weight_row[:, lanes]
        to_end = (BLOCK - 1 - iota((BLOCK, BLOCK), 0)).astype(F32)
        fade_high, fade_low = split(jnp.exp(-rate * to_end))
        fades = jnp.concatenate([fade_high, fade_high, fade_low], axis=0)
        later = (BLOCK * (blocks - 1 - iota((blocks, BLOCK), 0))).astype(F32)
        block_fade = jnp.exp(-rate * later)
        rows = slice(g * HALF, (g + 1) * HALF)
        total = jnp.zeros((HALF, BLOCK), F32)
        for copy in loads[g]:
            copy.wait()
        for start in range(0, blocks, 16):
            mixed = jnp.concatenate(
                [
                    key_ref[rows, b * BLOCK : (b + 1) * BLOCK] * value_ref[rows, b * BLOCK : (b + 1) * BLOCK]
                    for b in range(start, start + 16)
                ],
                axis=0,
            )
            mixed_ref[g, start * HALF : (start + 16) * HALF, :] = mixed
            high, low = split(mixed)
            states = lax.dot_general(
                jnp.concatenate([high, low, high], axis=1), fades, NN, preferred_element_type=F32
            )
            state_ref[g, start * HALF : (start + 16) * HALF, :] = states
            for b in range(16):
                total = total + block_fade[start + b : start + b + 1, :] * states[b * HALF : (b + 1) * HALF, :]
        end_ref[here, :] = jnp.sum(jnp.where(own, total, 0.0), axis=0, keepdims=True)
    query_load.wait()


def weight_tables(side, length, rate_ref, far_ref, enter_ref, leave_ref):
    me = lax.axis_index("ctx")
    place, inner = me % side, (me >= side) & (me < 3 * side)
    member = iota((2 * side, BLOCK), 0)
    own_part = member // side == lax.axis_index("chan") % 2
    source = jnp.where(inner, side + member, me - place + member % side)
    counted = (source < me) & (inner | own_part)
    handed = inner & (member < side)
    groups = rate_ref.shape[0]
    for g in range(groups):
        here = slice(g, g + 1)
        rate = rate_ref[here, :]
        passed = -rate * float(length)
        far_ref[here, :] = jnp.exp(passed * place.astype(F32))

        def faded(wanted, steps):
            return jnp.where(wanted, jnp.exp(passed * jnp.maximum(steps, 0).astype(F32)), 0.0)

        tables = (
            (enter_ref, 0, faded(counted, me - 1 - source)),
            (enter_ref, 1, faded(handed, me - 1 - member)),
            (leave_ref, 0, faded(member >= 0, 2 * side - 1 - member)),
            (leave_ref, 1, faded(member < side, 3 * side - 1 - member)),
        )
        for target, part, table in tables:
            for j in range(2 * side):
                target[j, part * groups + g : part * groups + g + 1, :] = table[j : j + 1, :]


def local_kernel(g, modes, side, length, mixed_ref, state_ref, skip_ref, rate_ref, weight_ref, base_ref, enter_ref, lead_ref, fade_ref, *rest):
    conv_rows = rest[-1]
    if rest[:-1]:
        weight_tables(side, length, rate_ref, *rest[:-1])
    blocks = base_ref.shape[0] // HALF
    square = (BLOCK, BLOCK)
    own = iota((HALF, BLOCK), 1) // modes == iota((HALF, BLOCK), 0)
    causal = iota(square, 1) >= iota(square, 0)
    rate = rate_ref[g : g + 1, :]
    gain = weight_ref[g : g + 1, :] * jnp.sqrt(one_minus_exp(2.0 * rate))
    lead_high, lead_low = split(gain * jnp.exp(-rate * (iota(square, 0).astype(F32) + 1.0)))
    lead_ref[...] = jnp.concatenate([lead_high, lead_high, lead_low], axis=1)
    fade_ref[...] = jnp.exp(-rate * (BLOCK * iota((blocks, BLOCK), 0)).astype(F32))
    tail = gain * jnp.exp(-rate * iota(square, 0).astype(F32))
    taps = lax.dot_general(
        own.astype(F32), tail, NT, precision=lax.Precision.HIGHEST, preferred_element_type=F32
    )
    step = jnp.exp(-rate * float(BLOCK))
    state = jnp.zeros((HALF, BLOCK), F32)
    for b in range(blocks):
        some = slice(b * HALF, (b + 1) * HALF)
        enter_ref[some, :] = jnp.where(own, state, 0.0)
        state = state * step + state_ref[g, some, :]
    for c in range(HALF):
        shifted = pltpu.roll(jnp.broadcast_to(taps[c : c + 1, :], square), 0, 1, stride=1, stride_axis=0)
        weights = jnp.concatenate(split(jnp.where(causal, shifted, 0.0)), axis=1)
        signal = jnp.concatenate(split(mixed_ref[g, pl.ds(c, blocks, stride=HALF), :]), axis=0)
        parts = lax.dot_general(signal, weights, NN, preferred_element_type=F32)
        conv_rows[pl.ds(c, blocks, stride=HALF), :] = parts[:blocks, :BLOCK] + (
            parts[:blocks, BLOCK:] + parts[blocks:, :BLOCK]
        )
    skip = skip_ref[g * HALF : (g + 1) * HALF, :]
    for b in range(blocks):
        some = slice(b * HALF, (b + 1) * HALF)
        base_ref[some, :] = conv_rows[some, :] + skip * mixed_ref[g, some, :]


def output_kernel(
    modes, query_ref, far_ref, near_ref, carried_ref, *rest
):
    groups = far_ref.shape[0]
    bases, enters, lead_refs, fade_refs = (rest[i * groups : (i + 1) * groups] for i in range(4))
    out_hbm, out_ref, sems = rest[4 * groups :]
    channels, length = query_ref.shape
    blocks = length // BLOCK
    own = iota((HALF, BLOCK), 1) // modes == iota((HALF, BLOCK), 0)
    stores = []
    for g in range(groups):
        rows = slice(g * HALF, (g + 1) * HALF)
        here = slice(g, g + 1)
        leads = lead_refs[g][...]
        entered = near_ref[here, :] + far_ref[here, :] * carried_ref[here, :]
        fades = entered * fade_refs[g][...]
        for start in range(0, blocks, 16):
            some = slice(start * HALF, (start + 16) * HALF)
            added = jnp.concatenate(
                [jnp.where(own, fades[b : b + 1, :], 0.0) for b in range(start, start + 16)], axis=0
            )
            high, low = split(enters[g][some, :] + added)
            conv = bases[g][some, :] + lax.dot_general(
                jnp.concatenate([high, low, high], axis=1), leads, NT, preferred_element_type=F32
            )
            for b in range(16):
                lanes = slice((start + b) * BLOCK, (start + b + 1) * BLOCK)
                out_ref[rows, lanes] = query_ref[rows, lanes] * conv[b * HALF : (b + 1) * HALF, :]
            lanes = slice(start * BLOCK, (start + 16) * BLOCK)
            store = pltpu.make_async_copy(out_ref.at[rows, lanes], out_hbm.at[rows, lanes], sems.at[len(stores)])
            store.start()
            stores.append(store)
    for store in stores:
        store.wait()


VMEM = pl.BlockSpec(memory_space=pltpu.VMEM)
HBM = pl.BlockSpec(memory_space=pltpu.HBM)
SIDE = 4


def shape(*dims):
    return jax.ShapeDtypeStruct(dims, F32)


def per_device(query_gate, key_gate, value_rows, filter_index, residues, decay_rates, skip_gain):
    channels, length = key_gate.shape
    modes = residues.shape[1]
    blocks = length // BLOCK
    groups = channels // HALF
    line = (groups, BLOCK)
    stripes = (groups, blocks * HALF, BLOCK)
    ends, rate, weight, skip, mixed, state, query = pl.pallas_call(
        state_kernel,
        out_shape=(
            shape(*line), shape(*line), shape(*line),
            shape(channels, BLOCK), shape(*stripes), shape(*stripes), shape(channels, length),
        ),
        in_specs=[HBM] * 7,
        out_specs=(VMEM,) * 7,
        scratch_shapes=[
            pltpu.VMEM((1, channels), jnp.int32),
            pltpu.VMEM((modes, residues.shape[0]), F32),
            pltpu.VMEM((modes, residues.shape[0]), F32),
            pltpu.VMEM((1, channels), F32),
            pltpu.VMEM((channels, length), F32),
            pltpu.VMEM((channels, length), F32),
            pltpu.SemaphoreType.DMA((2 * groups + 5,)),
        ],
        compiler_params=pltpu.CompilerParams(vmem_limit_bytes=16 * 2**20),
        cost_estimate=pl.CostEstimate(flops=2 * 3 * 1024 * 128 * 128, bytes_accessed=2**20, transcendentals=2**16),
    )(
        *(
            pltpu.with_memory_space_constraint(array, pltpu.HBM)
            for array in (
                filter_index.reshape(1, channels), decay_rates.T, residues.T, skip_gain.reshape(1, channels),
                key_gate, value_rows, query_gate,
            )
        )
    )

    tables = (shape(*line), shape(2 * SIDE, 2 * groups, BLOCK), shape(2 * SIDE, 2 * groups, BLOCK))

    def local(g, more=()):
        return pl.pallas_call(
            lambda *refs: local_kernel(g, modes, SIDE, length, *refs),
            out_shape=(
                shape(*stripes[1:]),
                shape(*stripes[1:]),
                jax.ShapeDtypeStruct((BLOCK, 3 * BLOCK), BF16),
                shape(blocks, BLOCK),
                *more,
            ),
            in_specs=[VMEM] * 5,
            out_specs=(VMEM,) * (4 + len(more)),
            scratch_shapes=[pltpu.VMEM(stripes[1:], F32)],
            compiler_params=pltpu.CompilerParams(vmem_limit_bytes=16 * 2**20),
            cost_estimate=pl.CostEstimate(flops=2 * 4 * 512 * 128 * 128, bytes_accessed=2**19, transcendentals=2**14),
        )(mixed, state, skip, rate, weight)

    parts = lax.axis_size("chan")
    inner = [[d * parts + part for d in range(SIDE, 3 * SIDE)] for part in range(parts)]
    outer = [
        [(row + x) * parts + pair + core for core in range(2) for x in range(SIDE)]
        for row in (0, 3 * SIDE)
        for pair in range(0, parts, 2)
    ]
    handed = lax.ppermute(ends, "ctx", [(x, SIDE + x) for x in range(SIDE)])
    handed, local_first, local_second = lax.optimization_barrier((handed, local(0, tables), local(1)))
    far, enter, leave = local_first[4:]
    own = jnp.concatenate([ends, handed], axis=0).reshape(1, 1, -1)
    every = lax.all_to_all(
        jnp.broadcast_to(own, (2 * SIDE, 1, own.size)),
        ("ctx", "chan"),
        split_axis=0,
        concat_axis=0,
        tiled=True,
        axis_index_groups=inner + outer,
    )
    every = every.reshape(2 * SIDE, 2 * groups, BLOCK)
    near = jnp.sum((enter * every).reshape(4 * SIDE, *line), axis=0)
    sent = jnp.sum((leave * every).reshape(4 * SIDE, *line), axis=0)
    carried = lax.ppermute(sent, "ctx", [(2 * SIDE + x, 3 * SIDE + x) for x in range(SIDE)])

    return pl.pallas_call(
        lambda *refs: output_kernel(modes, *refs),
        out_shape=shape(channels, length),
        in_specs=[VMEM] * (4 + 4 * groups),
        out_specs=HBM,
        scratch_shapes=[pltpu.VMEM((channels, length), F32), pltpu.SemaphoreType.DMA((groups * blocks // 16,))],
        compiler_params=pltpu.CompilerParams(vmem_limit_bytes=16 * 2**20),
        cost_estimate=pl.CostEstimate(flops=2 * 3 * 1024 * 128 * 128, bytes_accessed=2**21, transcendentals=2**16),
    )(query, far, near, carried, *(made[i] for i in range(4) for made in (local_first, local_second)))


def solution(mesh):
    placed = (P("chan", "ctx"), P("chan", "ctx"), P("chan", "ctx"), P("chan"), P(), P(), P("chan"))
    return jax.shard_map(
        per_device, mesh=mesh, in_specs=placed, out_specs=P("chan", "ctx"), check_vma=False
    )
```

```python
import jax
import jax.numpy as jnp
from jax import lax
from jax.experimental import pallas as pl
from jax.experimental.pallas import tpu as pltpu
from jax.sharding import PartitionSpec as P

BLOCK = 128
HALF = 8
F32, BF16 = jnp.float32, jnp.bfloat16
NN = (((1,), (0,)), ((), ()))
NT = (((1,), (1,)), ((), ()))


def split(value):
    high = value.astype(BF16)
    return high, (value - high.astype(F32)).astype(BF16)


def iota(shape, dim):
    return lax.broadcasted_iota(jnp.int32, shape, dim)


def one_minus_exp(x):
    series = jnp.full_like(x, 1.0)
    for k in range(9, 1, -1):
        series = 1.0 - x * series * (1.0 / k)
    return jnp.where(x <= 0.25, x * series, 1.0 - jnp.exp(-x))


def state_kernel(
    index_hbm, rates_hbm, residues_hbm, skip_hbm, key_hbm, value_hbm, query_hbm,
    end_ref, rate_ref, weight_ref, skip_ref, mixed_ref, state_ref, query_ref,
    index_ref, rates_ref, residues_ref, skip_row, key_ref, value_ref, sems,
):
    channels, length = key_ref.shape
    modes, filters = rates_ref.shape
    blocks = length // BLOCK
    groups = channels // HALF
    small = [
        pltpu.make_async_copy(source, target, sems.at[2 * groups + 1 + i])
        for i, (source, target) in enumerate(
            ((index_hbm, index_ref), (rates_hbm, rates_ref), (residues_hbm, residues_ref), (skip_hbm, skip_row))
        )
    ]
    for copy in small:
        copy.start()
    loads = []
    for g in range(groups):
        rows = slice(g * HALF, (g + 1) * HALF)
        pair = [
            pltpu.make_async_copy(source.at[rows, :], target.at[rows, :], sems.at[2 * g + i])
            for i, (source, target) in enumerate(((key_hbm, key_ref), (value_hbm, value_ref)))
        ]
        for copy in pair:
            copy.start()
        loads.append(pair)
    query_load = pltpu.make_async_copy(query_hbm, query_ref, sems.at[2 * groups])
    query_load.start()
    for copy in small:
        copy.wait()

    wide = (channels, channels * modes)
    spread = (iota(wide, 1) // modes == iota(wide, 0)).astype(BF16)
    chosen = (iota((filters, channels), 0) == index_ref[...]).astype(BF16)
    chosen = lax.dot_general(chosen, spread, NN, preferred_element_type=F32)
    own_mode = iota((modes, channels * modes), 1) % modes == iota((modes, channels * modes), 0)

    def lanes_of(table):
        spread_table = lax.dot_general(
            table, chosen, NN, precision=lax.Precision.HIGHEST, preferred_element_type=F32
        )
        return jnp.sum(jnp.where(own_mode, spread_table, 0.0), axis=0, keepdims=True)

    rate_row = lanes_of(rates_ref[...])
    weight_row = lanes_of(residues_ref[...])
    own = iota((HALF, BLOCK), 1) // modes == iota((HALF, BLOCK), 0)
    same = iota((channels, channels), 0) == iota((channels, channels), 1)
    skip = jnp.sum(jnp.where(same, skip_row[...], 0.0), axis=1, keepdims=True)
    skip_ref[...] = jnp.broadcast_to(skip, skip_ref.shape)
    for g in range(groups):
        lanes = slice(g * BLOCK, (g + 1) * BLOCK)
        rate = rate_row[:, lanes]
        here = slice(g, g + 1)
        rate_ref[here, :] = rate
        weight_ref[here, :] = weight_row[:, lanes]
        to_end = (BLOCK - 1 - iota((BLOCK, BLOCK), 0)).astype(F32)
        fade_high, fade_low = split(jnp.exp(-rate * to_end))
        fades = jnp.concatenate([fade_high, fade_high, fade_low], axis=0)
        later = (BLOCK * (blocks - 1 - iota((blocks, BLOCK), 0))).astype(F32)
        block_fade = jnp.exp(-rate * later)
        rows = slice(g * HALF, (g + 1) * HALF)
        total = jnp.zeros((HALF, BLOCK), F32)
        for copy in loads[g]:
            copy.wait()
        for start in range(0, blocks, 16):
            mixed = jnp.concatenate(
                [
                    key_ref[rows, b * BLOCK : (b + 1) * BLOCK] * value_ref[rows, b * BLOCK : (b + 1) * BLOCK]
                    for b in range(start, start + 16)
                ],
                axis=0,
            )
            mixed_ref[g, start * HALF : (start + 16) * HALF, :] = mixed
            high, low = split(mixed)
            states = lax.dot_general(
                jnp.concatenate([high, low, high], axis=1), fades, NN, preferred_element_type=F32
            )
            state_ref[g, start * HALF : (start + 16) * HALF, :] = states
            for b in range(16):
                total = total + block_fade[start + b : start + b + 1, :] * states[b * HALF : (b + 1) * HALF, :]
        end_ref[here, :] = jnp.sum(jnp.where(own, total, 0.0), axis=0, keepdims=True)
    query_load.wait()


def weight_tables(side, length, rate_ref, far_ref, enter_ref, leave_ref):
    me = lax.axis_index("ctx")
    place, inner = me % side, (me >= side) & (me < 3 * side)
    member = iota((2 * side, BLOCK), 0)
    own_part = member // side == lax.axis_index("chan") % 2
    source = jnp.where(inner, side + member, me - place + member % side)
    counted = (source < me) & (inner | own_part)
    handed = inner & (member < side)
    groups = rate_ref.shape[0]
    for g in range(groups):
        here = slice(g, g + 1)
        rate = rate_ref[here, :]
        passed = -rate * float(length)
        far_ref[here, :] = jnp.exp(passed * place.astype(F32))

        def faded(wanted, steps):
            return jnp.where(wanted, jnp.exp(passed * jnp.maximum(steps, 0).astype(F32)), 0.0)

        tables = (
            (enter_ref, 0, faded(counted, me - 1 - source)),
            (enter_ref, 1, faded(handed, me - 1 - member)),
            (leave_ref, 0, faded(member >= 0, 2 * side - 1 - member)),
            (leave_ref, 1, faded(member < side, 3 * side - 1 - member)),
        )
        for target, part, table in tables:
            for j in range(2 * side):
                target[j, part * groups + g : part * groups + g + 1, :] = table[j : j + 1, :]


def local_kernel(g, modes, side, length, mixed_ref, state_ref, skip_ref, rate_ref, weight_ref, base_ref, enter_ref, lead_ref, fade_ref, *rest):
    conv_rows = rest[-1]
    if rest[:-1]:
        weight_tables(side, length, rate_ref, *rest[:-1])
    blocks = base_ref.shape[0] // HALF
    square = (BLOCK, BLOCK)
    own = iota((HALF, BLOCK), 1) // modes == iota((HALF, BLOCK), 0)
    causal = iota(square, 1) >= iota(square, 0)
    rate = rate_ref[g : g + 1, :]
    gain = weight_ref[g : g + 1, :] * jnp.sqrt(one_minus_exp(2.0 * rate))
    lead_high, lead_low = split(gain * jnp.exp(-rate * (iota(square, 0).astype(F32) + 1.0)))
    lead_ref[...] = jnp.concatenate([lead_high, lead_high, lead_low], axis=1)
    fade_ref[...] = jnp.exp(-rate * (BLOCK * iota((blocks, BLOCK), 0)).astype(F32))
    tail = gain * jnp.exp(-rate * iota(square, 0).astype(F32))
    taps = lax.dot_general(
        own.astype(F32), tail, NT, precision=lax.Precision.HIGHEST, preferred_element_type=F32
    )
    step = jnp.exp(-rate * float(BLOCK))
    state = jnp.zeros((HALF, BLOCK), F32)
    for b in range(blocks):
        some = slice(b * HALF, (b + 1) * HALF)
        enter_ref[some, :] = jnp.where(own, state, 0.0)
        state = state * step + state_ref[g, some, :]
    for c in range(HALF):
        shifted = pltpu.roll(jnp.broadcast_to(taps[c : c + 1, :], square), 0, 1, stride=1, stride_axis=0)
        weights = jnp.concatenate(split(jnp.where(causal, shifted, 0.0)), axis=1)
        signal = jnp.concatenate(split(mixed_ref[g, pl.ds(c, blocks, stride=HALF), :]), axis=0)
        parts = lax.dot_general(signal, weights, NN, preferred_element_type=F32)
        conv_rows[pl.ds(c, blocks, stride=HALF), :] = parts[:blocks, :BLOCK] + (
            parts[:blocks, BLOCK:] + parts[blocks:, :BLOCK]
        )
    skip = skip_ref[g * HALF : (g + 1) * HALF, :]
    for b in range(blocks):
        some = slice(b * HALF, (b + 1) * HALF)
        base_ref[some, :] = conv_rows[some, :] + skip * mixed_ref[g, some, :]


def output_kernel(
    modes, query_ref, far_ref, near_ref, carried_ref, *rest
):
    groups = far_ref.shape[0]
    bases, enters, lead_refs, fade_refs = (rest[i * groups : (i + 1) * groups] for i in range(4))
    out_hbm, out_ref, sems = rest[4 * groups :]
    channels, length = query_ref.shape
    blocks = length // BLOCK
    own = iota((HALF, BLOCK), 1) // modes == iota((HALF, BLOCK), 0)
    stores = []
    for g in range(groups):
        rows = slice(g * HALF, (g + 1) * HALF)
        here = slice(g, g + 1)
        leads = lead_refs[g][...]
        entered = near_ref[here, :] + far_ref[here, :] * carried_ref[here, :]
        fades = entered * fade_refs[g][...]
        for start in range(0, blocks, 16):
            some = slice(start * HALF, (start + 16) * HALF)
            added = jnp.concatenate(
                [jnp.where(own, fades[b : b + 1, :], 0.0) for b in range(start, start + 16)], axis=0
            )
            high, low = split(enters[g][some, :] + added)
            conv = bases[g][some, :] + lax.dot_general(
                jnp.concatenate([high, low, high], axis=1), leads, NT, preferred_element_type=F32
            )
            for b in range(16):
                lanes = slice((start + b) * BLOCK, (start + b + 1) * BLOCK)
                out_ref[rows, lanes] = query_ref[rows, lanes] * conv[b * HALF : (b + 1) * HALF, :]
            lanes = slice(start * BLOCK, (start + 16) * BLOCK)
            store = pltpu.make_async_copy(out_ref.at[rows, lanes], out_hbm.at[rows, lanes], sems.at[len(stores)])
            store.start()
            stores.append(store)
    for store in stores:
        store.wait()


VMEM = pl.BlockSpec(memory_space=pltpu.VMEM)
HBM = pl.BlockSpec(memory_space=pltpu.HBM)
SIDE = 4


def shape(*dims):
    return jax.ShapeDtypeStruct(dims, F32)


def per_device(query_gate, key_gate, value_rows, filter_index, residues, decay_rates, skip_gain):
    channels, length = key_gate.shape
    modes = residues.shape[1]
    blocks = length // BLOCK
    groups = channels // HALF
    line = (groups, BLOCK)
    stripes = (groups, blocks * HALF, BLOCK)
    ends, rate, weight, skip, mixed, state, query = pl.pallas_call(
        state_kernel,
        out_shape=(
            shape(*line), shape(*line), shape(*line),
            shape(channels, BLOCK), shape(*stripes), shape(*stripes), shape(channels, length),
        ),
        in_specs=[HBM] * 7,
        out_specs=(VMEM,) * 7,
        scratch_shapes=[
            pltpu.VMEM((1, channels), jnp.int32),
            pltpu.VMEM((modes, residues.shape[0]), F32),
            pltpu.VMEM((modes, residues.shape[0]), F32),
            pltpu.VMEM((1, channels), F32),
            pltpu.VMEM((channels, length), F32),
            pltpu.VMEM((channels, length), F32),
            pltpu.SemaphoreType.DMA((2 * groups + 5,)),
        ],
        compiler_params=pltpu.CompilerParams(vmem_limit_bytes=16 * 2**20),
        cost_estimate=pl.CostEstimate(flops=2 * 3 * 1024 * 128 * 128, bytes_accessed=2**20, transcendentals=2**16),
    )(
        *(
            pltpu.with_memory_space_constraint(array, pltpu.HBM)
            for array in (
                filter_index.reshape(1, channels), decay_rates.T, residues.T, skip_gain.reshape(1, channels),
                key_gate, value_rows, query_gate,
            )
        )
    )

    tables = (shape(*line), shape(2 * SIDE, 2 * groups, BLOCK), shape(2 * SIDE, 2 * groups, BLOCK))

    def local(g, more=()):
        return pl.pallas_call(
            lambda *refs: local_kernel(g, modes, SIDE, length, *refs),
            out_shape=(
                shape(*stripes[1:]),
                shape(*stripes[1:]),
                jax.ShapeDtypeStruct((BLOCK, 3 * BLOCK), BF16),
                shape(blocks, BLOCK),
                *more,
            ),
            in_specs=[VMEM] * 5,
            out_specs=(VMEM,) * (4 + len(more)),
            scratch_shapes=[pltpu.VMEM(stripes[1:], F32)],
            compiler_params=pltpu.CompilerParams(vmem_limit_bytes=16 * 2**20),
            cost_estimate=pl.CostEstimate(flops=2 * 4 * 512 * 128 * 128, bytes_accessed=2**19, transcendentals=2**14),
        )(mixed, state, skip, rate, weight)

    parts = lax.axis_size("chan")
    inner = [[d * parts + part for d in range(SIDE, 3 * SIDE)] for part in range(parts)]
    outer = [
        [(row + x) * parts + pair + core for core in range(2) for x in range(SIDE)]
        for row in (0, 3 * SIDE)
        for pair in range(0, parts, 2)
    ]
    handed = lax.ppermute(ends, "ctx", [(x, SIDE + x) for x in range(SIDE)])
    handed, local_first, local_second = lax.optimization_barrier((handed, local(0, tables), local(1)))
    far, enter, leave = local_first[4:]
    own = jnp.concatenate([ends, handed], axis=0)
    every = lax.all_gather(own, ("ctx", "chan"), axis_index_groups=inner + outer)
    near = jnp.sum((enter * every).reshape(4 * SIDE, *line), axis=0)
    sent = jnp.sum((leave * every).reshape(4 * SIDE, *line), axis=0)
    carried = lax.ppermute(sent, "ctx", [(2 * SIDE + x, 3 * SIDE + x) for x in range(SIDE)])

    return pl.pallas_call(
        lambda *refs: output_kernel(modes, *refs),
        out_shape=shape(channels, length),
        in_specs=[VMEM] * (4 + 4 * groups),
        out_specs=HBM,
        scratch_shapes=[pltpu.VMEM((channels, length), F32), pltpu.SemaphoreType.DMA((groups * blocks // 16,))],
        compiler_params=pltpu.CompilerParams(vmem_limit_bytes=16 * 2**20),
        cost_estimate=pl.CostEstimate(flops=2 * 3 * 1024 * 128 * 128, bytes_accessed=2**21, transcendentals=2**16),
    )(query, far, near, carried, *(made[i] for i in range(4) for made in (local_first, local_second)))


def solution(mesh):
    placed = (P("chan", "ctx"), P("chan", "ctx"), P("chan", "ctx"), P("chan"), P(), P(), P("chan"))
    return jax.shard_map(
        per_device, mesh=mesh, in_specs=placed, out_specs=P("chan", "ctx"), check_vma=False
    )
```

```python
import jax
import jax.numpy as jnp
from jax import lax
from jax.experimental import pallas as pl
from jax.experimental.pallas import tpu as pltpu
from jax.sharding import PartitionSpec as P

BLOCK = 128
HALF = 8
F32, BF16 = jnp.float32, jnp.bfloat16
NN = (((1,), (0,)), ((), ()))
NT = (((1,), (1,)), ((), ()))


def split(value):
    high = value.astype(BF16)
    return high, (value - high.astype(F32)).astype(BF16)


def iota(shape, dim):
    return lax.broadcasted_iota(jnp.int32, shape, dim)


def one_minus_exp(x):
    series = jnp.full_like(x, 1.0)
    for k in range(9, 1, -1):
        series = 1.0 - x * series * (1.0 / k)
    return jnp.where(x <= 0.25, x * series, 1.0 - jnp.exp(-x))


def state_kernel(
    index_hbm, rates_hbm, residues_hbm, skip_hbm, key_hbm, value_hbm,
    end_ref, rate_ref, weight_ref, skip_ref, mixed_ref, state_ref,
    index_ref, rates_ref, residues_ref, skip_row, key_ref, value_ref, sems,
):
    channels, length = key_ref.shape
    modes, filters = rates_ref.shape
    blocks = length // BLOCK
    groups = channels // HALF
    small = [
        pltpu.make_async_copy(source, target, sems.at[2 * groups + i])
        for i, (source, target) in enumerate(
            ((index_hbm, index_ref), (rates_hbm, rates_ref), (residues_hbm, residues_ref), (skip_hbm, skip_row))
        )
    ]
    for copy in small:
        copy.start()
    loads = []
    for g in range(groups):
        rows = slice(g * HALF, (g + 1) * HALF)
        pair = [
            pltpu.make_async_copy(source.at[rows, :], target.at[rows, :], sems.at[2 * g + i])
            for i, (source, target) in enumerate(((key_hbm, key_ref), (value_hbm, value_ref)))
        ]
        for copy in pair:
            copy.start()
        loads.append(pair)
    for copy in small:
        copy.wait()

    wide = (channels, channels * modes)
    spread = (iota(wide, 1) // modes == iota(wide, 0)).astype(BF16)
    chosen = (iota((filters, channels), 0) == index_ref[...]).astype(BF16)
    chosen = lax.dot_general(chosen, spread, NN, preferred_element_type=F32)
    own_mode = iota((modes, channels * modes), 1) % modes == iota((modes, channels * modes), 0)

    def lanes_of(table):
        spread_table = lax.dot_general(
            table, chosen, NN, precision=lax.Precision.HIGHEST, preferred_element_type=F32
        )
        return jnp.sum(jnp.where(own_mode, spread_table, 0.0), axis=0, keepdims=True)

    rate_row = lanes_of(rates_ref[...])
    weight_row = lanes_of(residues_ref[...])
    own = iota((HALF, BLOCK), 1) // modes == iota((HALF, BLOCK), 0)
    same = iota((channels, channels), 0) == iota((channels, channels), 1)
    skip = jnp.sum(jnp.where(same, skip_row[...], 0.0), axis=1, keepdims=True)
    skip_ref[...] = jnp.broadcast_to(skip, skip_ref.shape)
    for g in range(groups):
        lanes = slice(g * BLOCK, (g + 1) * BLOCK)
        rate = rate_row[:, lanes]
        here = slice(g, g + 1)
        rate_ref[here, :] = rate
        weight_ref[here, :] = weight_row[:, lanes]
        to_end = (BLOCK - 1 - iota((BLOCK, BLOCK), 0)).astype(F32)
        fade_high, fade_low = split(jnp.exp(-rate * to_end))
        fades = jnp.concatenate([fade_high, fade_high, fade_low], axis=0)
        later = (BLOCK * (blocks - 1 - iota((blocks, BLOCK), 0))).astype(F32)
        block_fade = jnp.exp(-rate * later)
        rows = slice(g * HALF, (g + 1) * HALF)
        total = jnp.zeros((HALF, BLOCK), F32)
        for copy in loads[g]:
            copy.wait()
        for start in range(0, blocks, 16):
            mixed = jnp.concatenate(
                [
                    key_ref[rows, b * BLOCK : (b + 1) * BLOCK] * value_ref[rows, b * BLOCK : (b + 1) * BLOCK]
                    for b in range(start, start + 16)
                ],
                axis=0,
            )
            mixed_ref[g, start * HALF : (start + 16) * HALF, :] = mixed
            high, low = split(mixed)
            states = lax.dot_general(
                jnp.concatenate([high, low, high], axis=1), fades, NN, preferred_element_type=F32
            )
            state_ref[g, start * HALF : (start + 16) * HALF, :] = states
            for b in range(16):
                total = total + block_fade[start + b : start + b + 1, :] * states[b * HALF : (b + 1) * HALF, :]
        end_ref[here, :] = jnp.sum(jnp.where(own, total, 0.0), axis=0, keepdims=True)


def weight_tables(side, length, rate_ref, far_ref, enter_ref, leave_ref):
    me = lax.axis_index("ctx")
    place, inner = me % side, (me >= side) & (me < 3 * side)
    member = iota((2 * side, BLOCK), 0)
    own_part = member // side == lax.axis_index("chan") % 2
    source = jnp.where(inner, side + member, me - place + member % side)
    counted = (source < me) & (inner | own_part)
    handed = inner & (member < side)
    groups = rate_ref.shape[0]
    for g in range(groups):
        here = slice(g, g + 1)
        rate = rate_ref[here, :]
        passed = -rate * float(length)
        far_ref[here, :] = jnp.exp(passed * place.astype(F32))

        def faded(wanted, steps):
            return jnp.where(wanted, jnp.exp(passed * jnp.maximum(steps, 0).astype(F32)), 0.0)

        tables = (
            (enter_ref, 0, faded(counted, me - 1 - source)),
            (enter_ref, 1, faded(handed, me - 1 - member)),
            (leave_ref, 0, faded(member >= 0, 2 * side - 1 - member)),
            (leave_ref, 1, faded(member < side, 3 * side - 1 - member)),
        )
        for target, part, table in tables:
            for j in range(2 * side):
                target[j, part * groups + g : part * groups + g + 1, :] = table[j : j + 1, :]


def local_kernel(g, modes, side, length, mixed_ref, state_ref, skip_ref, rate_ref, weight_ref, base_ref, enter_ref, lead_ref, fade_ref, *rest):
    conv_rows = rest[-1]
    if rest[:-1]:
        weight_tables(side, length, rate_ref, *rest[:-1])
    blocks = base_ref.shape[0] // HALF
    square = (BLOCK, BLOCK)
    own = iota((HALF, BLOCK), 1) // modes == iota((HALF, BLOCK), 0)
    causal = iota(square, 1) >= iota(square, 0)
    rate = rate_ref[g : g + 1, :]
    gain = weight_ref[g : g + 1, :] * jnp.sqrt(one_minus_exp(2.0 * rate))
    lead_high, lead_low = split(gain * jnp.exp(-rate * (iota(square, 0).astype(F32) + 1.0)))
    lead_ref[...] = jnp.concatenate([lead_high, lead_high, lead_low], axis=1)
    fade_ref[...] = jnp.exp(-rate * (BLOCK * iota((blocks, BLOCK), 0)).astype(F32))
    tail = gain * jnp.exp(-rate * iota(square, 0).astype(F32))
    taps = lax.dot_general(
        own.astype(F32), tail, NT, precision=lax.Precision.HIGHEST, preferred_element_type=F32
    )
    step = jnp.exp(-rate * float(BLOCK))
    state = jnp.zeros((HALF, BLOCK), F32)
    for b in range(blocks):
        some = slice(b * HALF, (b + 1) * HALF)
        enter_ref[some, :] = jnp.where(own, state, 0.0)
        state = state * step + state_ref[g, some, :]
    for c in range(HALF):
        shifted = pltpu.roll(jnp.broadcast_to(taps[c : c + 1, :], square), 0, 1, stride=1, stride_axis=0)
        weights = jnp.concatenate(split(jnp.where(causal, shifted, 0.0)), axis=1)
        signal = jnp.concatenate(split(mixed_ref[g, pl.ds(c, blocks, stride=HALF), :]), axis=0)
        parts = lax.dot_general(signal, weights, NN, preferred_element_type=F32)
        conv_rows[pl.ds(c, blocks, stride=HALF), :] = parts[:blocks, :BLOCK] + (
            parts[:blocks, BLOCK:] + parts[blocks:, :BLOCK]
        )
    skip = skip_ref[g * HALF : (g + 1) * HALF, :]
    for b in range(blocks):
        some = slice(b * HALF, (b + 1) * HALF)
        base_ref[some, :] = conv_rows[some, :] + skip * mixed_ref[g, some, :]


def opening_kernel(modes, side, length, *refs):
    query_hbm, query_ref, sem = refs[5], refs[13], refs[15]
    load = pltpu.make_async_copy(query_hbm, query_ref, sem)
    load.start()
    local_kernel(0, modes, side, length, *refs[:5], *refs[6:13], refs[14])
    load.wait()


def output_kernel(
    modes, query_ref, far_ref, near_ref, carried_ref, *rest
):
    groups = far_ref.shape[0]
    bases, enters, lead_refs, fade_refs = (rest[i * groups : (i + 1) * groups] for i in range(4))
    out_hbm, out_ref, sems = rest[4 * groups :]
    channels, length = query_ref.shape
    blocks = length // BLOCK
    own = iota((HALF, BLOCK), 1) // modes == iota((HALF, BLOCK), 0)
    stores = []
    for g in range(groups):
        rows = slice(g * HALF, (g + 1) * HALF)
        here = slice(g, g + 1)
        leads = lead_refs[g][...]
        entered = near_ref[here, :] + far_ref[here, :] * carried_ref[here, :]
        fades = entered * fade_refs[g][...]
        for start in range(0, blocks, 16):
            some = slice(start * HALF, (start + 16) * HALF)
            added = jnp.concatenate(
                [jnp.where(own, fades[b : b + 1, :], 0.0) for b in range(start, start + 16)], axis=0
            )
            high, low = split(enters[g][some, :] + added)
            conv = bases[g][some, :] + lax.dot_general(
                jnp.concatenate([high, low, high], axis=1), leads, NT, preferred_element_type=F32
            )
            for b in range(16):
                lanes = slice((start + b) * BLOCK, (start + b + 1) * BLOCK)
                out_ref[rows, lanes] = query_ref[rows, lanes] * conv[b * HALF : (b + 1) * HALF, :]
            lanes = slice(start * BLOCK, (start + 16) * BLOCK)
            store = pltpu.make_async_copy(out_ref.at[rows, lanes], out_hbm.at[rows, lanes], sems.at[len(stores)])
            store.start()
            stores.append(store)
    for store in stores:
        store.wait()


VMEM = pl.BlockSpec(memory_space=pltpu.VMEM)
HBM = pl.BlockSpec(memory_space=pltpu.HBM)
SIDE = 4


def shape(*dims):
    return jax.ShapeDtypeStruct(dims, F32)


def per_device(query_gate, key_gate, value_rows, filter_index, residues, decay_rates, skip_gain):
    channels, length = key_gate.shape
    modes = residues.shape[1]
    blocks = length // BLOCK
    groups = channels // HALF
    line = (groups, BLOCK)
    stripes = (groups, blocks * HALF, BLOCK)
    ends, rate, weight, skip, mixed, state = pl.pallas_call(
        state_kernel,
        out_shape=(
            shape(*line), shape(*line), shape(*line),
            shape(channels, BLOCK), shape(*stripes), shape(*stripes),
        ),
        in_specs=[HBM] * 6,
        out_specs=(VMEM,) * 6,
        scratch_shapes=[
            pltpu.VMEM((1, channels), jnp.int32),
            pltpu.VMEM((modes, residues.shape[0]), F32),
            pltpu.VMEM((modes, residues.shape[0]), F32),
            pltpu.VMEM((1, channels), F32),
            pltpu.VMEM((channels, length), F32),
            pltpu.VMEM((channels, length), F32),
            pltpu.SemaphoreType.DMA((2 * groups + 4,)),
        ],
        compiler_params=pltpu.CompilerParams(vmem_limit_bytes=16 * 2**20),
        cost_estimate=pl.CostEstimate(flops=2 * 3 * 1024 * 128 * 128, bytes_accessed=2**20, transcendentals=2**16),
    )(
        *(
            pltpu.with_memory_space_constraint(array, pltpu.HBM)
            for array in (
                filter_index.reshape(1, channels), decay_rates.T, residues.T, skip_gain.reshape(1, channels),
                key_gate, value_rows,
            )
        )
    )

    weights = shape(2 * SIDE, 2 * groups, BLOCK)
    opening = (shape(*line), weights, weights, shape(channels, length))
    query_here = pltpu.with_memory_space_constraint(query_gate, pltpu.HBM)

    def local(g, more=()):
        kernel = opening_kernel if more else lambda *refs: local_kernel(g, *refs)
        return pl.pallas_call(
            lambda *refs: kernel(modes, SIDE, length, *refs),
            out_shape=(
                shape(*stripes[1:]),
                shape(*stripes[1:]),
                jax.ShapeDtypeStruct((BLOCK, 3 * BLOCK), BF16),
                shape(blocks, BLOCK),
                *more,
            ),
            in_specs=[VMEM] * 5 + [HBM] * bool(more),
            out_specs=(VMEM,) * (4 + len(more)),
            scratch_shapes=[pltpu.VMEM(stripes[1:], F32)] + [pltpu.SemaphoreType.DMA] * bool(more),
            compiler_params=pltpu.CompilerParams(vmem_limit_bytes=16 * 2**20),
            cost_estimate=pl.CostEstimate(flops=2 * 4 * 512 * 128 * 128, bytes_accessed=2**19, transcendentals=2**14),
        )(mixed, state, skip, rate, weight, *((query_here,) if more else ()))

    parts = lax.axis_size("chan")
    inner = [[d * parts + part for d in range(SIDE, 3 * SIDE)] for part in range(parts)]
    outer = [
        [(row + x) * parts + pair + core for core in range(2) for x in range(SIDE)]
        for row in (0, 3 * SIDE)
        for pair in range(0, parts, 2)
    ]
    handed = lax.ppermute(ends, "ctx", [(x, SIDE + x) for x in range(SIDE)])
    handed, local_first, local_second = lax.optimization_barrier((handed, local(0, opening), local(1)))
    far, enter, leave, query = local_first[4:]
    own = jnp.concatenate([ends, handed], axis=0).reshape(1, 1, -1)
    every = lax.all_to_all(
        jnp.broadcast_to(own, (2 * SIDE, 1, own.size)),
        ("ctx", "chan"),
        split_axis=0,
        concat_axis=0,
        tiled=True,
        axis_index_groups=inner + outer,
    )
    every = every.reshape(2 * SIDE, 2 * groups, BLOCK)
    near = jnp.sum((enter * every).reshape(4 * SIDE, *line), axis=0)
    sent = jnp.sum((leave * every).reshape(4 * SIDE, *line), axis=0)
    carried = lax.ppermute(sent, "ctx", [(2 * SIDE + x, 3 * SIDE + x) for x in range(SIDE)])

    return pl.pallas_call(
        lambda *refs: output_kernel(modes, *refs),
        out_shape=shape(channels, length),
        in_specs=[VMEM] * (4 + 4 * groups),
        out_specs=HBM,
        scratch_shapes=[pltpu.VMEM((channels, length), F32), pltpu.SemaphoreType.DMA((groups * blocks // 16,))],
        compiler_params=pltpu.CompilerParams(vmem_limit_bytes=16 * 2**20),
        cost_estimate=pl.CostEstimate(flops=2 * 3 * 1024 * 128 * 128, bytes_accessed=2**21, transcendentals=2**16),
    )(query, far, near, carried, *(made[i] for i in range(4) for made in (local_first, local_second)))


def solution(mesh):
    placed = (P("chan", "ctx"), P("chan", "ctx"), P("chan", "ctx"), P("chan"), P(), P(), P("chan"))
    return jax.shard_map(
        per_device, mesh=mesh, in_specs=placed, out_specs=P("chan", "ctx"), check_vma=False
    )
```

```python
import jax
import jax.numpy as jnp
from jax import lax
from jax.experimental import pallas as pl
from jax.experimental.pallas import tpu as pltpu
from jax.sharding import PartitionSpec as P

BLOCK = 128
HALF = 8
F32, BF16 = jnp.float32, jnp.bfloat16
NN = (((1,), (0,)), ((), ()))
NT = (((1,), (1,)), ((), ()))


def split(value):
    high = value.astype(BF16)
    return high, (value - high.astype(F32)).astype(BF16)


def iota(shape, dim):
    return lax.broadcasted_iota(jnp.int32, shape, dim)


def one_minus_exp(x):
    series = jnp.full_like(x, 1.0)
    for k in range(9, 1, -1):
        series = 1.0 - x * series * (1.0 / k)
    return jnp.where(x <= 0.25, x * series, 1.0 - jnp.exp(-x))


def state_kernel(
    index_hbm, rates_hbm, residues_hbm, skip_hbm, key_hbm, value_hbm, query_hbm,
    end_ref, rate_ref, weight_ref, skip_ref, mixed_ref, state_ref, query_ref,
    index_ref, rates_ref, residues_ref, skip_row, key_ref, value_ref, sems,
):
    channels, length = key_ref.shape
    modes, filters = rates_ref.shape
    blocks = length // BLOCK
    groups = channels // HALF
    small = [
        pltpu.make_async_copy(source, target, sems.at[2 * groups + 1 + i])
        for i, (source, target) in enumerate(
            ((index_hbm, index_ref), (rates_hbm, rates_ref), (residues_hbm, residues_ref), (skip_hbm, skip_row))
        )
    ]
    for copy in small:
        copy.start()
    loads = []
    for g in range(groups):
        rows = slice(g * HALF, (g + 1) * HALF)
        pair = [
            pltpu.make_async_copy(source.at[rows, :], target.at[rows, :], sems.at[2 * g + i])
            for i, (source, target) in enumerate(((key_hbm, key_ref), (value_hbm, value_ref)))
        ]
        for copy in pair:
            copy.start()
        loads.append(pair)
    query_load = pltpu.make_async_copy(query_hbm, query_ref, sems.at[2 * groups])
    query_load.start()
    for copy in small:
        copy.wait()

    wide = (channels, channels * modes)
    spread = (iota(wide, 1) // modes == iota(wide, 0)).astype(BF16)
    chosen = (iota((filters, channels), 0) == index_ref[...]).astype(BF16)
    chosen = lax.dot_general(chosen, spread, NN, preferred_element_type=F32)
    own_mode = iota((modes, channels * modes), 1) % modes == iota((modes, channels * modes), 0)

    def lanes_of(table):
        spread_table = lax.dot_general(
            table, chosen, NN, precision=lax.Precision.HIGHEST, preferred_element_type=F32
        )
        return jnp.sum(jnp.where(own_mode, spread_table, 0.0), axis=0, keepdims=True)

    rate_row = lanes_of(rates_ref[...])
    weight_row = lanes_of(residues_ref[...])
    own = iota((HALF, BLOCK), 1) // modes == iota((HALF, BLOCK), 0)
    same = iota((channels, channels), 0) == iota((channels, channels), 1)
    skip = jnp.sum(jnp.where(same, skip_row[...], 0.0), axis=1, keepdims=True)
    skip_ref[...] = jnp.broadcast_to(skip, skip_ref.shape)
    for g in range(groups):
        lanes = slice(g * BLOCK, (g + 1) * BLOCK)
        rate = rate_row[:, lanes]
        here = slice(g, g + 1)
        rate_ref[here, :] = rate
        weight_ref[here, :] = weight_row[:, lanes]
        to_end = (BLOCK - 1 - iota((BLOCK, BLOCK), 0)).astype(F32)
        fade_high, fade_low = split(jnp.exp(-rate * to_end))
        fades = jnp.concatenate([fade_high, fade_high, fade_low], axis=0)
        later = (BLOCK * (blocks - 1 - iota((blocks, BLOCK), 0))).astype(F32)
        block_fade = jnp.exp(-rate * later)
        rows = slice(g * HALF, (g + 1) * HALF)
        total = jnp.zeros((HALF, BLOCK), F32)
        for copy in loads[g]:
            copy.wait()
        for start in range(0, blocks, 16):
            mixed = jnp.concatenate(
                [
                    key_ref[rows, b * BLOCK : (b + 1) * BLOCK] * value_ref[rows, b * BLOCK : (b + 1) * BLOCK]
                    for b in range(start, start + 16)
                ],
                axis=0,
            )
            mixed_ref[g, start * HALF : (start + 16) * HALF, :] = mixed
            high, low = split(mixed)
            states = lax.dot_general(
                jnp.concatenate([high, low, high], axis=1), fades, NN, preferred_element_type=F32
            )
            state_ref[g, start * HALF : (start + 16) * HALF, :] = states
            for b in range(16):
                total = total + block_fade[start + b : start + b + 1, :] * states[b * HALF : (b + 1) * HALF, :]
        end_ref[here, :] = jnp.sum(jnp.where(own, total, 0.0), axis=0, keepdims=True)
    query_load.wait()


def weight_tables(side, length, rate_ref, far_ref, enter_ref, leave_ref):
    me = lax.axis_index("ctx")
    place, inner = me % side, (me >= side) & (me < 3 * side)
    member = iota((2 * side, BLOCK), 0)
    own_part = member // side == lax.axis_index("chan") % 2
    source = jnp.where(inner, side + member, me - place + member % side)
    counted = (source < me) & (inner | own_part)
    handed = inner & (member < side)
    groups = rate_ref.shape[0]
    for g in range(groups):
        here = slice(g, g + 1)
        rate = rate_ref[here, :]
        passed = -rate * float(length)
        far_ref[here, :] = jnp.exp(passed * place.astype(F32))

        def faded(wanted, steps):
            return jnp.where(wanted, jnp.exp(passed * jnp.maximum(steps, 0).astype(F32)), 0.0)

        tables = (
            (enter_ref, 0, faded(counted, me - 1 - source)),
            (enter_ref, 1, faded(handed, me - 1 - member)),
            (leave_ref, 0, faded(member >= 0, 2 * side - 1 - member)),
            (leave_ref, 1, faded(member < side, 3 * side - 1 - member)),
        )
        for target, part, table in tables:
            for j in range(2 * side):
                target[j, part * groups + g : part * groups + g + 1, :] = table[j : j + 1, :]


def local_kernel(g, modes, side, length, mixed_ref, state_ref, skip_ref, rate_ref, weight_ref, base_ref, enter_ref, lead_ref, fade_ref, *rest):
    conv_rows = rest[-1]
    if rest[:-1]:
        weight_tables(side, length, rate_ref, *rest[:-1])
    blocks = base_ref.shape[0] // HALF
    square = (BLOCK, BLOCK)
    own = iota((HALF, BLOCK), 1) // modes == iota((HALF, BLOCK), 0)
    causal = iota(square, 1) >= iota(square, 0)
    rate = rate_ref[g : g + 1, :]
    gain = weight_ref[g : g + 1, :] * jnp.sqrt(one_minus_exp(2.0 * rate))
    lead_high, lead_low = split(gain * jnp.exp(-rate * (iota(square, 0).astype(F32) + 1.0)))
    lead_ref[...] = jnp.concatenate([lead_high, lead_high, lead_low], axis=1)
    fade_ref[...] = jnp.exp(-rate * (BLOCK * iota((blocks, BLOCK), 0)).astype(F32))
    tail = gain * jnp.exp(-rate * iota(square, 0).astype(F32))
    taps = lax.dot_general(
        own.astype(F32), tail, NT, precision=lax.Precision.HIGHEST, preferred_element_type=F32
    )
    step = jnp.exp(-rate * float(BLOCK))
    state = jnp.zeros((HALF, BLOCK), F32)
    for b in range(blocks):
        some = slice(b * HALF, (b + 1) * HALF)
        enter_ref[some, :] = jnp.where(own, state, 0.0)
        state = state * step + state_ref[g, some, :]
    for c in range(HALF):
        shifted = pltpu.roll(jnp.broadcast_to(taps[c : c + 1, :], square), 0, 1, stride=1, stride_axis=0)
        weights = jnp.concatenate(split(jnp.where(causal, shifted, 0.0)), axis=1)
        signal = jnp.concatenate(split(mixed_ref[g, pl.ds(c, blocks, stride=HALF), :]), axis=0)
        parts = lax.dot_general(signal, weights, NN, preferred_element_type=F32)
        conv_rows[pl.ds(c, blocks, stride=HALF), :] = parts[:blocks, :BLOCK] + (
            parts[:blocks, BLOCK:] + parts[blocks:, :BLOCK]
        )
    skip = skip_ref[g * HALF : (g + 1) * HALF, :]
    for b in range(blocks):
        some = slice(b * HALF, (b + 1) * HALF)
        base_ref[some, :] = conv_rows[some, :] + skip * mixed_ref[g, some, :]


def output_kernel(
    modes, query_ref, far_ref, near_ref, carried_ref, *rest
):
    groups = far_ref.shape[0]
    bases, enters, lead_refs, fade_refs = (rest[i * groups : (i + 1) * groups] for i in range(4))
    out_hbm, out_ref, sems = rest[4 * groups :]
    channels, length = query_ref.shape
    blocks = length // BLOCK
    own = iota((HALF, BLOCK), 1) // modes == iota((HALF, BLOCK), 0)
    stores = []
    for g in range(groups):
        rows = slice(g * HALF, (g + 1) * HALF)
        here = slice(g, g + 1)
        leads = lead_refs[g][...]
        entered = near_ref[here, :] + far_ref[here, :] * carried_ref[here, :]
        fades = entered * fade_refs[g][...]
        for start in range(0, blocks, 8):
            some = slice(start * HALF, (start + 8) * HALF)
            added = jnp.concatenate(
                [jnp.where(own, fades[b : b + 1, :], 0.0) for b in range(start, start + 8)], axis=0
            )
            high, low = split(enters[g][some, :] + added)
            conv = bases[g][some, :] + lax.dot_general(
                jnp.concatenate([high, low, high], axis=1), leads, NT, preferred_element_type=F32
            )
            for b in range(8):
                lanes = slice((start + b) * BLOCK, (start + b + 1) * BLOCK)
                out_ref[rows, lanes] = query_ref[rows, lanes] * conv[b * HALF : (b + 1) * HALF, :]
            lanes = slice(start * BLOCK, (start + 8) * BLOCK)
            store = pltpu.make_async_copy(out_ref.at[rows, lanes], out_hbm.at[rows, lanes], sems.at[len(stores)])
            store.start()
            stores.append(store)
    for store in stores:
        store.wait()


VMEM = pl.BlockSpec(memory_space=pltpu.VMEM)
HBM = pl.BlockSpec(memory_space=pltpu.HBM)
SIDE = 4


def shape(*dims):
    return jax.ShapeDtypeStruct(dims, F32)


def per_device(query_gate, key_gate, value_rows, filter_index, residues, decay_rates, skip_gain):
    channels, length = key_gate.shape
    modes = residues.shape[1]
    blocks = length // BLOCK
    groups = channels // HALF
    line = (groups, BLOCK)
    stripes = (groups, blocks * HALF, BLOCK)
    ends, rate, weight, skip, mixed, state, query = pl.pallas_call(
        state_kernel,
        out_shape=(
            shape(*line), shape(*line), shape(*line),
            shape(channels, BLOCK), shape(*stripes), shape(*stripes), shape(channels, length),
        ),
        in_specs=[HBM] * 7,
        out_specs=(VMEM,) * 7,
        scratch_shapes=[
            pltpu.VMEM((1, channels), jnp.int32),
            pltpu.VMEM((modes, residues.shape[0]), F32),
            pltpu.VMEM((modes, residues.shape[0]), F32),
            pltpu.VMEM((1, channels), F32),
            pltpu.VMEM((channels, length), F32),
            pltpu.VMEM((channels, length), F32),
            pltpu.SemaphoreType.DMA((2 * groups + 5,)),
        ],
        compiler_params=pltpu.CompilerParams(vmem_limit_bytes=16 * 2**20),
        cost_estimate=pl.CostEstimate(flops=2 * 3 * 1024 * 128 * 128, bytes_accessed=2**20, transcendentals=2**16),
    )(
        *(
            pltpu.with_memory_space_constraint(array, pltpu.HBM)
            for array in (
                filter_index.reshape(1, channels), decay_rates.T, residues.T, skip_gain.reshape(1, channels),
                key_gate, value_rows, query_gate,
            )
        )
    )

    tables = (shape(*line), shape(2 * SIDE, 2 * groups, BLOCK), shape(2 * SIDE, 2 * groups, BLOCK))

    def local(g, more=()):
        return pl.pallas_call(
            lambda *refs: local_kernel(g, modes, SIDE, length, *refs),
            out_shape=(
                shape(*stripes[1:]),
                shape(*stripes[1:]),
                jax.ShapeDtypeStruct((BLOCK, 3 * BLOCK), BF16),
                shape(blocks, BLOCK),
                *more,
            ),
            in_specs=[VMEM] * 5,
            out_specs=(VMEM,) * (4 + len(more)),
            scratch_shapes=[pltpu.VMEM(stripes[1:], F32)],
            compiler_params=pltpu.CompilerParams(vmem_limit_bytes=16 * 2**20),
            cost_estimate=pl.CostEstimate(flops=2 * 4 * 512 * 128 * 128, bytes_accessed=2**19, transcendentals=2**14),
        )(mixed, state, skip, rate, weight)

    parts = lax.axis_size("chan")
    inner = [[d * parts + part for d in range(SIDE, 3 * SIDE)] for part in range(parts)]
    outer = [
        [(row + x) * parts + pair + core for core in range(2) for x in range(SIDE)]
        for row in (0, 3 * SIDE)
        for pair in range(0, parts, 2)
    ]
    handed = lax.ppermute(ends, "ctx", [(x, SIDE + x) for x in range(SIDE)])
    handed, local_first, local_second = lax.optimization_barrier((handed, local(0, tables), local(1)))
    far, enter, leave = local_first[4:]
    own = jnp.concatenate([ends, handed], axis=0).reshape(1, 1, -1)
    every = lax.all_to_all(
        jnp.broadcast_to(own, (2 * SIDE, 1, own.size)),
        ("ctx", "chan"),
        split_axis=0,
        concat_axis=0,
        tiled=True,
        axis_index_groups=inner + outer,
    )
    every = every.reshape(2 * SIDE, 2 * groups, BLOCK)
    near = jnp.sum((enter * every).reshape(4 * SIDE, *line), axis=0)
    sent = jnp.sum((leave * every).reshape(4 * SIDE, *line), axis=0)
    carried = lax.ppermute(sent, "ctx", [(2 * SIDE + x, 3 * SIDE + x) for x in range(SIDE)])

    return pl.pallas_call(
        lambda *refs: output_kernel(modes, *refs),
        out_shape=shape(channels, length),
        in_specs=[VMEM] * (4 + 4 * groups),
        out_specs=HBM,
        scratch_shapes=[pltpu.VMEM((channels, length), F32), pltpu.SemaphoreType.DMA((groups * blocks // 8,))],
        compiler_params=pltpu.CompilerParams(vmem_limit_bytes=16 * 2**20),
        cost_estimate=pl.CostEstimate(flops=2 * 3 * 1024 * 128 * 128, bytes_accessed=2**21, transcendentals=2**16),
    )(query, far, near, carried, *(made[i] for i in range(4) for made in (local_first, local_second)))


def solution(mesh):
    placed = (P("chan", "ctx"), P("chan", "ctx"), P("chan", "ctx"), P("chan"), P(), P(), P("chan"))
    return jax.shard_map(
        per_device, mesh=mesh, in_specs=placed, out_specs=P("chan", "ctx"), check_vma=False
    )
```
